256 devices in a mesh: ia: 8 (over z), ja: 8 (over x, core), ka: 4 (over y).
Axes of the slice: x: 4, y: 4, z: 8, core: 2. Of those that a mesh axis runs over, the one named last changes fastest.
Arguments:
- tensor: float32 [1024, 1024, 512], P('ia', 'ja', 'ka'), may hold values from -6000 to 6000
- factor_b: float32 [1024, 256], P(('ja', 'ia', 'ka')), may hold values from -6 to 6
- factor_c: float32 [512, 256], P(('ka', 'ia', 'ja')), may hold values from -6 to 6
Outputs:
- new_a: float32 [1024, 256], P(('ia', 'ja', 'ka'))
- new_b: float32 [1024, 256], P(('ja', 'ia', 'ka'))
- new_c: float32 [512, 256], P(('ka', 'ia', 'ja'))
The draws below stay inside these ranges and needn't reach their ends.
All inputs are finite; a program needn't handle non-finite values.
Results may differ from the reference program's by a relative error of at most 0.0003.
Values sent between devices are 32-bit elements; how exact they have to be, the bound alone decides.
A program may use at most 128 MiB of HBM per device.

```python
import jax
import jax.numpy as jnp
from jax import lax

I_BLK = 128
RANK = 256
NI = 1024
NJ = 1024
NK = 512


def shared_mixing(key):
    return jax.random.normal(jax.random.fold_in(key, 901), (16, RANK), jnp.float32) * 0.25


def mix_columns(base_rows, mixing, noise_part, noise_scale):
    combined = noise_part * noise_scale
    for source in range(16):
        combined = combined + base_rows[:, source:source + 1] * mixing[source:source + 1, :]
    return jnp.clip(combined, -6.0, 6.0)


def draw_factor_b(key, part):
    mixing = shared_mixing(key)
    key = jax.random.fold_in(key, 3)
    base_key, noise_key = jax.random.split(key)
    base_rows = jax.random.normal(base_key, (NJ, 16), jnp.float32)
    noise_part = jax.random.normal(noise_key, (NJ, RANK), jnp.float32)
    return mix_columns(base_rows, mixing, noise_part, 0.25)


def draw_factor_c(key, part):
    mixing = shared_mixing(key)
    key = jax.random.fold_in(key, 7)
    base_key, noise_key = jax.random.split(key)
    base_rows = jax.random.normal(base_key, (NK, 16), jnp.float32)
    noise_part = jax.random.normal(noise_key, (NK, RANK), jnp.float32)
    return mix_columns(base_rows, mixing, noise_part, 0.25)


def shard_levels(rng, dims, cuts, least, largest):
    level = 1.0
    for dim, blocks in cuts:
        draws = jax.random.uniform(jax.random.fold_in(jax.random.fold_in(rng, 6), dim), (blocks,), jnp.float32, least / len(cuts), largest / len(cuts))
        level = level * jnp.repeat(jnp.exp(draws), dims[dim] // blocks).reshape((-1,) + (1,) * (len(dims) - 1 - dim))
    return level


def bell_draw(key, dims, deviation, bound, shards=(), kind=jnp.bfloat16):
    array = deviation * jax.random.normal(key, dims, jnp.float32)
    if shards:
        array = array * shard_levels(key, dims, shards, -0.22, 0.18)
    return jnp.clip(array, -bound, bound).astype(kind)


def setup_inputs(seed: int = 0) -> dict:
    keys = jax.random.split(jax.random.key(seed), 4)
    return {
        "tensor": bell_draw(keys[0], (NI, NJ, NK), 1000.0, 6000.0, ((0, 8), (1, 8), (2, 4)), jnp.float32),
        "factor_b": draw_factor_b(jax.random.fold_in(keys[3], 71), 0),
        "factor_c": draw_factor_c(jax.random.fold_in(keys[3], 71), 0),
    }


def contract(form, left, right):
    return jnp.einsum(form, left, right, precision=lax.Precision.HIGHEST)

def gram_of(rows):
    return contract('nr,ns->rs', rows, rows)

def solve_rows(rows, hadamard):
    factor = jnp.linalg.cholesky(hadamard)
    return jax.scipy.linalg.cho_solve((factor, True), rows.T).T

def column_scale(gram_matrix, count):
    return jnp.sqrt(jnp.diagonal(gram_matrix) / count + 1e-06)

def reference(tensor, factor_b, factor_c):
    blocks = tensor.reshape(NI // I_BLK, I_BLK, NJ, NK)
    gram_b = gram_of(factor_b)
    gram_c = gram_of(factor_c)

    def mode_one(piece):
        return contract('ikr,kr->ir', contract('ijk,jr->ikr', piece, factor_b), factor_c)
    rows_a = lax.map(mode_one, blocks).reshape(NI, RANK)
    raw_a = solve_rows(rows_a, gram_b * gram_c)
    gram_ra = gram_of(raw_a)
    scale_a = column_scale(gram_ra, NI)
    new_a = raw_a / scale_a
    gram_a = gram_ra / (scale_a[:, None] * scale_a[None, :])
    a_blocks = new_a.reshape(NI // I_BLK, I_BLK, RANK)

    def add_b(total, pair):
        piece, arows = pair
        return (total + contract('ijr,ir->jr', contract('ijk,kr->ijr', piece, factor_c), arows), None)
    rows_b, _ = lax.scan(add_b, jnp.zeros((NJ, RANK), jnp.float32), (blocks, a_blocks))
    raw_b = solve_rows(rows_b, gram_a * gram_c)
    gram_rb = gram_of(raw_b)
    scale_b = column_scale(gram_rb, NJ)
    new_b = raw_b / scale_b
    gram_nb = gram_rb / (scale_b[:, None] * scale_b[None, :])

    def add_c(total, pair):
        piece, arows = pair
        return (total + contract('ikr,ir->kr', contract('ijk,jr->ikr', piece, new_b), arows), None)
    rows_c, _ = lax.scan(add_c, jnp.zeros((NK, RANK), jnp.float32), (blocks, a_blocks))
    raw_c = solve_rows(rows_c, gram_a * gram_nb)
    norms = lax.optimization_barrier(jnp.sum(raw_c * raw_c, axis=0))
    new_c = raw_c / jnp.sqrt(norms / NK + 1e-06)
    return (new_a, new_b, new_c)
```

```python
import functools

import jax
import jax.numpy as jnp
from jax import lax
from jax.experimental import pallas as pl
from jax.experimental.pallas import tpu as pltpu
from jax.sharding import PartitionSpec as P

MESH = pl.DeviceIdType.MESH
F32 = jnp.float32
BF16 = jnp.bfloat16
HIGHEST = lax.Precision.HIGHEST
PIV = 32
GROUP = 8


def split(v):
    hi = v.astype(BF16)
    lo = (v - hi.astype(F32)).astype(BF16)
    return hi, lo


def stack_split(v):
    hi, lo = split(v)
    return jnp.concatenate([hi, hi], axis=0), jnp.concatenate([lo, lo], axis=0)


def mxu(left, right):
    return jnp.dot(left, right, preferred_element_type=F32)


def dot_full(left, right):
    return jnp.dot(left, right, preferred_element_type=F32, precision=HIGHEST)


def gram_of(rows):
    return lax.dot_general(
        rows, rows, (((0,), (0,)), ((), ())), preferred_element_type=F32, precision=HIGHEST
    )


def diagonals(matrix):
    n = matrix.shape[0]
    row = lax.broadcasted_iota(jnp.int32, (n, n), 0)
    col = lax.broadcasted_iota(jnp.int32, (n, n), 1)
    only = jnp.where(row == col, matrix, 0.0)
    return jnp.sum(only, axis=0, keepdims=True), jnp.sum(only, axis=1, keepdims=True)


def sweep_step(mat):
    n = mat.shape[0]
    front = mat[0:PIV, :]
    panel = front
    sub = lax.broadcasted_iota(jnp.int32, (PIV, n), 0)
    lane = lax.broadcasted_iota(jnp.int32, (PIV, n), 1)
    for p in range(PIV):
        col = panel[:, p : p + 1]
        inverse = 1.0 / panel[p : p + 1, p : p + 1]
        unit = jnp.where(lane == p, jnp.where(sub == p, 1.0, 0.0), panel)
        row = unit[p : p + 1, :] * inverse
        panel = jnp.where(sub == p, row, unit - col * row)
    wide = jnp.concatenate([panel, jnp.zeros((128 - PIV, n), F32)], axis=0)
    tall = wide.T
    front_wide = jnp.concatenate([front, jnp.zeros((128 - PIV, n), F32)], axis=0)
    rest = mat[PIV:, :] - dot_full(tall[PIV:, :], front_wide)
    tall_wide = jnp.concatenate([tall[PIV:, :], jnp.zeros((n - PIV, n - 128), F32)], axis=1)
    rest_lane = lax.broadcasted_iota(jnp.int32, (n - PIV, n), 1)
    rest = jnp.where(rest_lane < PIV, tall_wide, rest)
    top = jnp.where(lane < PIV, -panel, panel)
    mat_new = jnp.concatenate([rest, top], axis=0)
    return pltpu.roll(mat_new, n - PIV, 1)


def invert_in(ref):
    n = ref.shape[0]

    def step(_, carry):
        ref[...] = sweep_step(ref[...])
        return carry

    lax.fori_loop(0, n // PIV, step, 0)


def kernel(
    ni, nj, nk, counts,
    x_hbm, b_ref, c_ref, oa_ref, ob_ref, oc_ref,
    xs, xt, ys, bin_, cin, bblk, cblk, ablk, nblk, whi, wlo, rows, arow,
    part_ab, part_b, part_c, recv_a, recv_b, recv_c, own_a, own_b, gat_a, gat_b,
    gp_b, gp_c, gp_a, gp_n, ex_b, ex_c, ex_a, ex_n, sum_b, sum_c, sum_a, sum_n,
    g_b, g_c, g_a, g_n, hmat, gca, nrm1, nrm2, own_n1, own_n2,
    ss, rs, xsem,
):
    rank = b_ref.shape[1]
    nblkrows = 128
    ia, ja, ka = lax.axis_index("ia"), lax.axis_index("ja"), lax.axis_index("ka")
    n_a, n_b, n_c, n_d = nj * nk, ni * nk, ni * nj, ni * nj // 2
    me_a, me_b, me_c, me_d = ja * nk + ka, ia * nk + ka, ia * nj + ja, ia * (nj // 2) + ja // 2

    def peer_a(q):
        return {"ia": ia, "ja": q // nk, "ka": lax.rem(q, nk)}

    def peer_b(q):
        return {"ia": q // nk, "ja": ja, "ka": lax.rem(q, nk)}

    def peer_c(q):
        return {"ia": q // nj, "ja": lax.rem(q, nj), "ka": ka}

    def peer_d(q):
        return {"ia": q // (nj // 2), "ja": lax.rem(q, nj // 2) * 2 + lax.rem(ja, 2), "ka": ka}

    def line_i(q):
        return {"ia": q, "ja": ja, "ka": ka}

    def line_j(q):
        return {"ia": ia, "ja": q, "ka": ka}

    def line_k(q):
        return {"ia": ia, "ja": ja, "ka": q}

    def send(phase, n, me, peer, src_of, dst):
        def go(p, carry):
            q = lax.rem(me + p, n)
            pltpu.make_async_remote_copy(
                src_ref=src_of(q), dst_ref=dst, send_sem=ss.at[phase], recv_sem=rs.at[phase],
                device_id=peer(q), device_id_type=MESH,
            ).start()
            return carry
        lax.fori_loop(1, n, go, 0)

    def all_of(phase, n, me, peer, buf):
        some = buf.at[pl.ds(0, n - 1)]
        return pltpu.make_async_remote_copy(
            src_ref=some, dst_ref=some, send_sem=ss.at[phase], recv_sem=rs.at[phase],
            device_id=peer(lax.rem(me + 1, n)), device_id_type=MESH,
        )

    def assemble(dst, src):
        n, per = src.shape[0], src.shape[1]
        for s in range(n):
            dst[s * per : (s + 1) * per, :] = src[s]

    def scatter_out(dst, src):
        n, per = dst.shape[0], dst.shape[1]
        for s in range(n):
            dst[s] = src[s * per : (s + 1) * per, :]

    xcopy = pltpu.make_async_copy(x_hbm, xs, xsem)
    xcopy.start()
    barrier = pltpu.get_barrier_semaphore()

    def hello(n, me, peer):
        def go(p, carry):
            pl.semaphore_signal(barrier, inc=1, device_id=peer(lax.rem(me + p, n)), device_id_type=MESH)
            return carry
        lax.fori_loop(1, n, go, 0)

    hello(n_a, me_a, peer_a)

    def other_i(p, carry):
        i2 = lax.rem(ia + p, ni)

        def along_j(j2, c2):
            pl.semaphore_signal(barrier, inc=1, device_id={"ia": i2, "ja": j2, "ka": ka}, device_id_type=MESH)
            return c2
        lax.fori_loop(0, nj, along_j, 0)

        def along_k(k2, c2):
            pl.semaphore_signal(
                barrier, inc=1, device_id={"ia": i2, "ja": ja, "ka": lax.rem(ka + k2, nk)}, device_id_type=MESH
            )
            return c2
        lax.fori_loop(1, nk, along_k, 0)
        return carry
    lax.fori_loop(1, ni, other_i, 0)
    pl.semaphore_wait(barrier, (n_a - 1) + (ni - 1) * (nj + nk - 1))

    bin_[me_b] = b_ref[...]
    cin[me_c] = c_ref[...]
    send(0, n_b, me_b, peer_b, lambda q: b_ref, bin_.at[me_b])
    send(1, n_c, me_c, peer_c, lambda q: c_ref, cin.at[me_c])

    xcopy.wait()

    def turn(j, carry):
        hi, lo = split(xs[pl.ds(j, nblkrows, stride=nblkrows), :].T)
        at = pl.ds(pl.multiple_of(j * nblkrows, nblkrows), nblkrows)
        xt[at, 0:128] = hi
        xt[at, 128:256] = lo
        return carry
    lax.fori_loop(0, 128, turn, 0, unroll=4)

    all_of(0, n_b, me_b, peer_b, bin_).wait_recv()
    all_of(1, n_c, me_c, peer_c, cin).wait_recv()
    assemble(bblk, bin_)
    assemble(cblk, cin)

    def gram_slices(dst, blk):
        dst[...] = gram_of(blk[...]).reshape(dst.shape)

    gram_slices(gp_b, bblk)
    gram_slices(gp_c, cblk)
    ex_b[ja] = gp_b[me_b]
    send(2, nj, ja, line_j, lambda q: gp_b.at[me_b], ex_b.at[ja])
    ex_c[ka] = gp_c[me_d]
    send(3, nk, ka, line_k, lambda q: gp_c.at[me_d], ex_c.at[ka])

    whi[...], wlo[...] = stack_split(cblk[...])
    step_rows = GROUP * nblkrows

    def mode_one(g, carry):
        at = pl.ds(pl.multiple_of(g * step_rows, step_rows), step_rows)
        hi, lo = split(xs[at, :])
        both = jnp.concatenate([hi, lo], axis=1)
        y = mxu(both, whi[...]) + mxu(both, wlo[...])
        ys[at, :] = y
        terms = y.reshape(GROUP, nblkrows, rank) * bblk[...][None]
        rows[pl.ds(pl.multiple_of(g * GROUP, GROUP), GROUP), :] = jnp.sum(terms, axis=1)
        return carry

    steps = 128 // GROUP
    lax.fori_loop(0, steps // 2, mode_one, 0)

    def finish_gram(phase, n, me, line, ex, own, n_p, me_p, peer, full):
        all_of(phase, n, me, line, ex).wait_recv()
        total = jnp.sum(ex[...], axis=0)
        own[...] = total
        full[me_p] = total
        send(phase + 2, n_p, me_p, peer, lambda q: own, full.at[me_p])

    finish_gram(2, nj, ja, line_j, ex_b, sum_b, n_b, me_b, peer_b, g_b)
    finish_gram(3, nk, ka, line_k, ex_c, sum_c, n_d, me_d, peer_d, g_c)
    lax.fori_loop(steps // 2, steps, mode_one, 0)

    scatter_out(part_ab, rows)
    recv_a[me_a] = part_ab[me_a]
    send(6, n_a, me_a, peer_a, lambda q: part_ab.at[q], recv_a.at[me_a])

    all_of(4, n_b, me_b, peer_b, g_b).wait_recv()
    all_of(5, n_d, me_d, peer_d, g_c).wait_recv()
    hmat[...] = g_b[...].reshape(rank, rank) * g_c[...].reshape(rank, rank)
    invert_in(hmat)

    def solve(summed):
        per = summed.shape[0]
        if per < 8:
            summed = jnp.concatenate([summed, jnp.zeros((8 - per, rank), F32)], axis=0)
        return -dot_full(summed, hmat[...])[0:per]

    all_of(6, n_a, me_a, peer_a, recv_a).wait_recv()
    own_a[...] = solve(jnp.sum(recv_a[...], axis=0))
    gat_a[me_a] = own_a[...]
    send(7, n_a, me_a, peer_a, lambda q: own_a, gat_a.at[me_a])
    all_of(7, n_a, me_a, peer_a, gat_a).wait_recv()
    assemble(ablk, gat_a)

    gram_slices(gp_a, ablk)
    ex_a[ia] = gp_a[me_a]
    send(8, ni, ia, line_i, lambda q: gp_a.at[me_a], ex_a.at[ia])

    def sum_rows(factor):
        def add(s, total):
            at = pl.ds(pl.multiple_of(s * nblkrows, nblkrows), nblkrows)
            return total + ys[at, :] * factor[pl.ds(s, 1), :]
        return lax.fori_loop(0, 128, add, jnp.zeros((nblkrows, rank), F32), unroll=8)

    rows[...] = sum_rows(ablk)
    scatter_out(part_b, rows)
    recv_b[me_b] = part_b[me_b]
    send(10, n_b, me_b, peer_b, lambda q: part_b.at[q], recv_b.at[me_b])

    all_of(8, ni, ia, line_i, ex_a).wait_recv()
    total_a = jnp.sum(ex_a[...], axis=0)
    sum_a[...] = total_a
    g_a[me_a] = total_a
    send(9, n_a, me_a, peer_a, lambda q: sum_a, g_a.at[me_a])

    whi[...], wlo[...] = stack_split(ablk[...])

    def third(g, carry):
        at = pl.ds(pl.multiple_of(g * step_rows, step_rows), step_rows)
        both = xt[at, :]
        ys[at, :] = mxu(both, whi[...]) + mxu(both, wlo[...])
        return carry
    lax.fori_loop(0, steps, third, 0)

    all_of(9, n_a, me_a, peer_a, g_a).wait_recv()
    gram = g_a[...].reshape(rank, rank)
    along, down = diagonals(gram)
    scale_a = jnp.sqrt(along / counts[0] + 1e-06)
    inverse_a = 1.0 / scale_a
    gca[...] = (gram * inverse_a) * (1.0 / jnp.sqrt(down / counts[0] + 1e-06))
    hmat[...] = gca[...] * g_c[...].reshape(rank, rank)
    oa_ref[...] = own_a[...] / scale_a
    arow[...] = inverse_a
    invert_in(hmat)

    all_of(10, n_b, me_b, peer_b, recv_b).wait_recv()
    own_b[...] = solve(jnp.sum(recv_b[...], axis=0) * arow[...])
    gat_b[me_b] = own_b[...]
    send(11, n_b, me_b, peer_b, lambda q: own_b, gat_b.at[me_b])
    all_of(11, n_b, me_b, peer_b, gat_b).wait_recv()
    assemble(nblk, gat_b)

    gram_slices(gp_n, nblk)
    ex_n[ja] = gp_n[me_b]
    send(12, nj, ja, line_j, lambda q: gp_n.at[me_b], ex_n.at[ja])

    nblk[...] = nblk[...] * arow[...]
    rows[...] = sum_rows(nblk)
    scatter_out(part_c, rows)
    recv_c[me_c] = part_c[me_c]
    send(14, n_c, me_c, peer_c, lambda q: part_c.at[q], recv_c.at[me_c])

    all_of(12, nj, ja, line_j, ex_n).wait_recv()
    total_n = jnp.sum(ex_n[...], axis=0)
    sum_n[...] = total_n
    g_n[me_b] = total_n
    send(13, n_b, me_b, peer_b, lambda q: sum_n, g_n.at[me_b])
    all_of(13, n_b, me_b, peer_b, g_n).wait_recv()
    gram = g_n[...].reshape(rank, rank)
    along, down = diagonals(gram)
    scale_b = jnp.sqrt(along / counts[1] + 1e-06)
    inverse_b = 1.0 / scale_b
    hmat[...] = gca[...] * ((gram * inverse_b) * (1.0 / jnp.sqrt(down / counts[1] + 1e-06)))
    ob_ref[...] = own_b[...] / scale_b
    arow[...] = inverse_b
    invert_in(hmat)

    all_of(14, n_c, me_c, peer_c, recv_c).wait_recv()
    raw_c = solve(jnp.sum(recv_c[...], axis=0) * arow[...])
    squares = jnp.sum(raw_c * raw_c, axis=0, keepdims=True)
    own_n1[...] = squares
    nrm1[ia] = squares
    send(15, ni, ia, line_i, lambda q: own_n1, nrm1.at[ia])
    all_of(15, ni, ia, line_i, nrm1).wait_recv()
    squares = jnp.sum(nrm1[...], axis=0)
    own_n2[...] = squares
    nrm2[me_a] = squares
    send(16, n_a, me_a, peer_a, lambda q: own_n2, nrm2.at[me_a])
    all_of(16, n_a, me_a, peer_a, nrm2).wait_recv()
    squares = jnp.sum(nrm2[...], axis=0)
    oc_ref[...] = raw_c / jnp.sqrt(squares / counts[2] + 1e-06)

    for phase, n, me, peer, buf in (
        (0, n_b, me_b, peer_b, bin_), (1, n_c, me_c, peer_c, cin),
        (2, nj, ja, line_j, ex_b), (3, nk, ka, line_k, ex_c),
        (4, n_b, me_b, peer_b, g_b), (5, n_d, me_d, peer_d, g_c),
        (6, n_a, me_a, peer_a, recv_a), (7, n_a, me_a, peer_a, gat_a),
        (8, ni, ia, line_i, ex_a), (9, n_a, me_a, peer_a, g_a),
        (10, n_b, me_b, peer_b, recv_b), (11, n_b, me_b, peer_b, gat_b),
        (12, nj, ja, line_j, ex_n), (13, n_b, me_b, peer_b, g_n),
        (14, n_c, me_c, peer_c, recv_c), (15, ni, ia, line_i, nrm1),
        (16, n_a, me_a, peer_a, nrm2),
    ):
        all_of(phase, n, me, peer, buf).wait_send()


def per_device(ni, nj, nk, tensor, factor_b, factor_c):
    counts = (tensor.shape[0] * ni, tensor.shape[1] * nj, tensor.shape[2] * nk)
    rank = factor_b.shape[1]
    n_a, n_b, n_c, n_d = nj * nk, ni * nk, ni * nj, ni * nj // 2
    r_a, r_b, r_c = 128 // n_a, 128 // n_b, 128 // n_c
    v = lambda *shape: pltpu.VMEM(shape, F32)
    scratch = [
        v(16384, 128), pltpu.VMEM((16384, 256), BF16), v(16384, rank),
        v(n_b, r_b, rank), v(n_c, r_c, rank),
        v(128, rank), v(128, rank), v(128, rank), v(128, rank),
        pltpu.VMEM((256, rank), BF16), pltpu.VMEM((256, rank), BF16),
        v(128, rank), v(1, rank),
        v(n_a, r_a, rank), v(n_b, r_b, rank), v(n_c, r_c, rank),
        v(n_a, r_a, rank), v(n_b, r_b, rank), v(n_c, r_c, rank),
        v(r_a, rank), v(r_b, rank), v(n_a, r_a, rank), v(n_b, r_b, rank),
        v(n_b, rank // n_b, rank), v(n_d, rank // n_d, rank),
        v(n_a, rank // n_a, rank), v(n_b, rank // n_b, rank),
        v(nj, rank // n_b, rank), v(nk, rank // n_d, rank),
        v(ni, rank // n_a, rank), v(nj, rank // n_b, rank),
        v(rank // n_b, rank), v(rank // n_d, rank), v(rank // n_a, rank), v(rank // n_b, rank),
        v(n_b, rank // n_b, rank), v(n_d, rank // n_d, rank),
        v(n_a, rank // n_a, rank), v(n_b, rank // n_b, rank),
        v(rank, rank), v(rank, rank),
        v(ni, 1, rank), v(n_a, 1, rank), v(1, rank), v(1, rank),
        pltpu.SemaphoreType.DMA((17,)), pltpu.SemaphoreType.DMA((17,)), pltpu.SemaphoreType.DMA,
    ]
    vmem = pl.BlockSpec(memory_space=pltpu.VMEM)
    return pl.pallas_call(
        functools.partial(kernel, ni, nj, nk, counts),
        out_shape=(
            jax.ShapeDtypeStruct((r_a, rank), F32),
            jax.ShapeDtypeStruct((r_b, rank), F32),
            jax.ShapeDtypeStruct((r_c, rank), F32),
        ),
        in_specs=[pl.BlockSpec(memory_space=pl.ANY), vmem, vmem],
        out_specs=(vmem, vmem, vmem),
        scratch_shapes=scratch,
        compiler_params=pltpu.CompilerParams(
            collective_id=0, has_side_effects=True, vmem_limit_bytes=52 * 1024 * 1024
        ),
    )(tensor.reshape(16384, 128), factor_b, factor_c)


def solution(mesh):
    ni, nj, nk = mesh.shape["ia"], mesh.shape["ja"], mesh.shape["ka"]
    return jax.shard_map(
        functools.partial(per_device, ni, nj, nk),
        mesh=mesh,
        in_specs=(P("ia", "ja", "ka"), P(("ja", "ia", "ka"), None), P(("ka", "ia", "ja"), None)),
        out_specs=(
            P(("ia", "ja", "ka"), None),
            P(("ja", "ia", "ka"), None),
            P(("ka", "ia", "ja"), None),
        ),
        check_vma=False,
    )
```

```python
import functools

import jax
import jax.numpy as jnp
from jax import lax
from jax.experimental import pallas as pl
from jax.experimental.pallas import tpu as pltpu
from jax.sharding import PartitionSpec as P

MESH = pl.DeviceIdType.MESH
F32 = jnp.float32
BF16 = jnp.bfloat16
HIGHEST = lax.Precision.HIGHEST
PIV = 32
GROUP = 8
SERVE = 4
SERVE_B = 4
SERVE_C = 3
TURNS = (32, 96)


def split(v):
    hi = v.astype(BF16)
    lo = (v - hi.astype(F32)).astype(BF16)
    return hi, lo


def stack_split(v):
    hi, lo = split(v)
    return jnp.concatenate([hi, hi], axis=0), jnp.concatenate([lo, lo], axis=0)


def mxu(left, right):
    return jnp.dot(left, right, preferred_element_type=F32)


def dot_full(left, right):
    return jnp.dot(left, right, preferred_element_type=F32, precision=HIGHEST)


def gram_of(rows):
    return lax.dot_general(
        rows, rows, (((0,), (0,)), ((), ())), preferred_element_type=F32, precision=HIGHEST
    )


def diagonals(matrix):
    n = matrix.shape[0]
    row = lax.broadcasted_iota(jnp.int32, (n, n), 0)
    col = lax.broadcasted_iota(jnp.int32, (n, n), 1)
    only = jnp.where(row == col, matrix, 0.0)
    return jnp.sum(only, axis=0, keepdims=True), jnp.sum(only, axis=1, keepdims=True)


def pivot_eight(rows, first):
    n = rows.shape[1]
    sub = lax.broadcasted_iota(jnp.int32, (8, 128), 0)
    lane = lax.broadcasted_iota(jnp.int32, (8, 128), 1)
    cols = [jnp.broadcast_to(rows[:, first + j : first + j + 1], (8, 128)) for j in range(8)]
    parts = [rows[:, h : h + 128] for h in range(0, n, 128)]
    for p in range(8):
        here = sub == p
        pivot = cols[p]
        inverse = 1.0 / jnp.broadcast_to(pivot[p : p + 1, :], (8, 128))
        parts[0] = jnp.where(lane == first + p, jnp.where(here, 1.0, 0.0), parts[0])

        def eliminate(v):
            scaled = jnp.broadcast_to(v[p : p + 1, :], (8, 128)) * inverse
            return jnp.where(here, scaled, v - pivot * scaled)

        parts = [eliminate(v) for v in parts]
        for j in range(p + 1, 8):
            cols[j] = eliminate(cols[j])
    return jnp.concatenate(parts, axis=1)


def pivot_panel(front):
    n = front.shape[1]
    groups = [front[g : g + 8, :] for g in range(0, PIV, 8)]
    lane = lax.broadcasted_iota(jnp.int32, (8, n), 1)
    for t in range(len(groups)):
        others = [g for g in range(len(groups)) if g != t]
        cols = {
            g: [jnp.broadcast_to(groups[g][:, 8 * t + j : 8 * t + j + 1], (8, n)) for j in range(8)]
            for g in others
        }
        groups[t] = pivot_eight(groups[t], 8 * t)
        wide = [jnp.broadcast_to(groups[t][j : j + 1, :], (8, n)) for j in range(8)]
        inside = (lane >= 8 * t) & (lane < 8 * t + 8)
        for g in others:
            terms = [cols[g][j] * wide[j] for j in range(8)]
            while len(terms) > 1:
                terms = [terms[i] + terms[i + 1] for i in range(0, len(terms), 2)]
            groups[g] = jnp.where(inside, 0.0, groups[g]) - terms[0]
    return jnp.concatenate(groups, axis=0)


def sweep_step(mat):
    n = mat.shape[0]
    front = mat[0:PIV, :]
    panel = pivot_panel(front)
    lane = lax.broadcasted_iota(jnp.int32, (PIV, n), 1)
    tall = jnp.concatenate([panel, jnp.zeros((128 - PIV, n), F32)], axis=0).T
    front_wide = jnp.concatenate([front, jnp.zeros((128 - PIV, n), F32)], axis=0)
    rest = mat[PIV:, :] - dot_full(tall[PIV:, :], front_wide)
    tall_wide = jnp.concatenate([tall[PIV:, :], jnp.zeros((n - PIV, n - 128), F32)], axis=1)
    rest_lane = lax.broadcasted_iota(jnp.int32, (n - PIV, n), 1)
    rest = jnp.where(rest_lane < PIV, tall_wide, rest)
    top = jnp.where(lane < PIV, -panel, panel)
    return pltpu.roll(jnp.concatenate([rest, top], axis=0), n - PIV, 1)


def invert_in(ref, first=0, last=None):
    def step(_, carry):
        ref[...] = sweep_step(ref[...])
        return carry

    lax.fori_loop(first, ref.shape[0] // PIV if last is None else last, step, 0)


def kernel(
    ni, nj, nk, counts,
    x_hbm, b_hbm, c_hbm, oa_ref, ob_ref, oc_ref,
    xs, xt, ys, bin_, cin, bblk, cblk, ablk, nblk, whi, wlo, rows, fac, arow,
    part_a, part_b, part_c, recv_a, recv_b, recv_c, own_a, own_b, own_c, gat_a, gat_b, gat_c,
    bx, cy, nx, half_b, half_c, half_n, other_b, other_c, other_n,
    gp_a, ex_a, sum_a, g_a, gcm, hmat, gca, nrm, own_n,
    ss, rs, xsem,
):
    rank = b_hbm.shape[1]
    nblkrows = 128
    ia, ja, ka = lax.axis_index("ia"), lax.axis_index("ja"), lax.axis_index("ka")
    n_a, n_b, n_c, nx_ = nj * nk, ni * nk, ni * nj, nj // 2
    me_a, me_b, me_c = ja * nk + ka, ia * nk + ka, ia * nj + ja
    x, core = ja // 2, lax.rem(ja, 2)

    def peer_a(q):
        return {"ia": ia, "ja": q // nk, "ka": lax.rem(q, nk)}

    def peer_b(q):
        return {"ia": q // nk, "ja": ja, "ka": lax.rem(q, nk)}

    def peer_c(q):
        return {"ia": q // nj, "ja": lax.rem(q, nj), "ka": ka}

    def line_i(q):
        return {"ia": q, "ja": ja, "ka": ka}

    def line_j(q):
        return {"ia": ia, "ja": q, "ka": ka}

    def line_k(q):
        return {"ia": ia, "ja": ja, "ka": q}

    started = []

    def line_x(q):
        return {"ia": ia, "ja": q * 2 + core, "ka": ka}

    def sibling(q):
        return {"ia": ia, "ja": x * 2 + q, "ka": ka}

    def send(phase, n, me, peer, src_of, dst, buf):
        started.append((phase, n, me, peer, buf))

        def go(p, carry):
            q = lax.rem(me + p, n)
            pltpu.make_async_remote_copy(
                src_ref=src_of(q), dst_ref=dst, send_sem=ss.at[phase], recv_sem=rs.at[phase],
                device_id=peer(q), device_id_type=MESH,
            ).start()
            return carry
        lax.fori_loop(1, n, go, 0)

    def all_of(phase, n, me, peer, buf):
        some = buf.at[pl.ds(0, n - 1)]
        return pltpu.make_async_remote_copy(
            src_ref=some, dst_ref=some, send_sem=ss.at[phase], recv_sem=rs.at[phase],
            device_id=peer(lax.rem(me + 1, n)), device_id_type=MESH,
        )

    def assemble(dst, src):
        per = src.shape[-2]
        count = dst.shape[0] // per
        inner = src.shape[1]
        for s in range(count):
            dst[s * per : (s + 1) * per, :] = src[s] if len(src.shape) == 3 else src[s // inner, s % inner]

    def scatter_out(dst, src):
        n, per = dst.shape[0], dst.shape[1]
        for s in range(n):
            dst[s] = src[s * per : (s + 1) * per, :]

    def own_rows(blk, me, per):
        if per >= 8:
            return blk[pl.ds(pl.multiple_of(me * per, 8), per), :]
        shared = 8 // per
        tile = blk[pl.ds(pl.multiple_of(me // shared * 8, 8), 8), :]
        mine = tile[0:per]
        for t in range(1, shared):
            mine = jnp.where(lax.rem(me, shared) == t, tile[t * per : (t + 1) * per], mine)
        return mine

    xcopy = pltpu.make_async_copy(x_hbm, xs, xsem.at[0])
    xcopy.start()
    bcopy = pltpu.make_async_copy(b_hbm, bin_.at[ia, ka], xsem.at[1])
    bcopy.start()
    ccopy = pltpu.make_async_copy(c_hbm, cin.at[ia, ja], xsem.at[2])
    ccopy.start()
    barrier = pltpu.get_barrier_semaphore()

    def hello(n, me, peer):
        def go(p, carry):
            pl.semaphore_signal(barrier, inc=1, device_id=peer(lax.rem(me + p, n)), device_id_type=MESH)
            return carry
        lax.fori_loop(1, n, go, 0)

    hello(ni, ia, line_i)
    hello(nj, ja, line_j)
    hello(nk, ka, line_k)

    def turn(j, carry):
        hi, lo = split(xs[pl.ds(j, nblkrows, stride=nblkrows), :].T)
        at = pl.ds(pl.multiple_of(j * nblkrows, nblkrows), nblkrows)
        xt[at, 0:128] = hi
        xt[at, 128:256] = lo
        return carry

    def turn_some(first, last):
        lax.fori_loop(first, last, turn, 0, unroll=4)

    bcopy.wait()
    ccopy.wait()
    xcopy.wait()
    turn_some(0, TURNS[0])
    pl.semaphore_wait(barrier, ni + nj + nk - 3)

    send(0, nk, ka, line_k, lambda q: bin_.at[ia, ka], bin_.at[ia, ka], bin_.at[ia])
    send(1, nj, ja, line_j, lambda q: cin.at[ia, ja], cin.at[ia, ja], cin.at[ia])
    turn_some(TURNS[0], TURNS[1])
    all_of(0, nk, ka, line_k, bin_.at[ia]).wait_recv()
    send(2, ni, ia, line_i, lambda q: bin_.at[ia], bin_.at[ia], bin_)
    all_of(1, nj, ja, line_j, cin.at[ia]).wait_recv()
    send(3, ni, ia, line_i, lambda q: cin.at[ia], cin.at[ia], cin)
    turn_some(TURNS[1], 128)
    all_of(2, ni, ia, line_i, bin_).wait_recv()
    assemble(bblk, bin_)
    bx[x] = bblk[...]
    send(4, nx_, x, line_x, lambda q: bblk, bx.at[x], bx)
    all_of(3, ni, ia, line_i, cin).wait_recv()
    assemble(cblk, cin)
    mine = pl.ds(pl.multiple_of(core * 64, 64), 64)
    cy[ka] = cblk[mine, :]
    send(5, nk, ka, line_k, lambda q: cblk.at[mine], cy.at[ka], cy)

    def gram_slices(dst, blk):
        dst[...] = gram_of(blk[...]).reshape(dst.shape)

    whi[...], wlo[...] = stack_split(cblk[...])
    step_rows = GROUP * nblkrows

    def mode_one(g, carry):
        at = pl.ds(pl.multiple_of(g * step_rows, step_rows), step_rows)
        hi, lo = split(xs[at, :])
        both = jnp.concatenate([hi, lo], axis=1)
        y = mxu(both, whi[...]) + mxu(both, wlo[...])
        ys[at, :] = y
        terms = y.reshape(GROUP, nblkrows, rank) * bblk[...][None]
        rows[pl.ds(pl.multiple_of(g * GROUP, GROUP), GROUP), :] = jnp.sum(terms, axis=1)
        return carry

    steps = 128 // GROUP
    lax.fori_loop(0, steps, mode_one, 0)

    scatter_out(part_a, rows)
    recv_a[me_a] = part_a[me_a]
    send(6, n_a, me_a, peer_a, lambda q: part_a.at[q], recv_a.at[me_a], recv_a)

    def swap(phase, half, other):
        send(phase, 2, core, sibling, lambda q: half, other.at[0], other)

    def swapped(phase, half, other):
        all_of(phase, 2, core, sibling, other).wait_recv()
        return half[...] + other[0]

    all_of(5, nk, ka, line_k, cy).wait_recv()
    half_c[...] = gram_of(cy[...].reshape(nk * 64, rank))
    swap(7, half_c, other_c)
    all_of(4, nx_, x, line_x, bx).wait_recv()
    half_b[...] = gram_of(bx[...].reshape(nx_ * 128, rank))
    swap(8, half_b, other_b)
    gcm[...] = swapped(7, half_c, other_c)
    hmat[...] = swapped(8, half_b, other_b) * gcm[...]
    invert_in(hmat, 0, SERVE)
    all_of(6, n_a, me_a, peer_a, recv_a).wait_recv()
    own_a[...] = jnp.sum(recv_a[...], axis=0)
    gat_a[me_a] = own_a[...]
    send(9, n_a, me_a, peer_a, lambda q: own_a, gat_a.at[me_a], gat_a)
    invert_in(hmat, SERVE)

    all_of(9, n_a, me_a, peer_a, gat_a).wait_recv()
    assemble(ablk, gat_a)
    ablk[...] = -dot_full(ablk[...], hmat[...])

    gram_slices(gp_a, ablk)
    ex_a[ia] = gp_a[me_a]
    send(10, ni, ia, line_i, lambda q: gp_a.at[me_a], ex_a.at[ia], ex_a)

    def sum_rows(factor):
        def add(s, total):
            at = pl.ds(pl.multiple_of(s * nblkrows, nblkrows), nblkrows)
            return total + ys[at, :] * factor[pl.ds(s, 1), :]
        return lax.fori_loop(0, 128, add, jnp.zeros((nblkrows, rank), F32), unroll=8)

    rows[...] = sum_rows(ablk)
    scatter_out(part_b, rows)
    recv_b[me_b] = part_b[me_b]
    send(12, n_b, me_b, peer_b, lambda q: part_b.at[q], recv_b.at[me_b], recv_b)

    whi[...], wlo[...] = stack_split(ablk[...])

    def third(g, carry):
        at = pl.ds(pl.multiple_of(g * step_rows, step_rows), step_rows)
        both = xt[at, :]
        ys[at, :] = mxu(both, whi[...]) + mxu(both, wlo[...])
        return carry
    lax.fori_loop(0, steps // 2, third, 0)
    all_of(10, ni, ia, line_i, ex_a).wait_recv()
    total_a = jnp.sum(ex_a[...], axis=0)
    sum_a[...] = total_a
    g_a[me_a] = total_a
    send(11, n_a, me_a, peer_a, lambda q: sum_a, g_a.at[me_a], g_a)

    lax.fori_loop(steps // 2, steps, third, 0)

    all_of(12, n_b, me_b, peer_b, recv_b).wait_recv()
    own_b[...] = jnp.sum(recv_b[...], axis=0)
    gat_b[me_b] = own_b[...]
    send(13, n_b, me_b, peer_b, lambda q: own_b, gat_b.at[me_b], gat_b)

    all_of(11, n_a, me_a, peer_a, g_a).wait_recv()
    gram = g_a[...].reshape(rank, rank)
    along, down = diagonals(gram)
    scale_a = jnp.sqrt(along / counts[0] + 1e-06)
    inverse_a = 1.0 / scale_a
    gca[...] = (gram * inverse_a) * (1.0 / jnp.sqrt(down / counts[0] + 1e-06))
    hmat[...] = gca[...] * gcm[...]
    oa_ref[...] = own_rows(ablk, me_a, oa_ref.shape[0]) / scale_a
    arow[...] = inverse_a
    invert_in(hmat, 0, SERVE_B)
    all_of(13, n_b, me_b, peer_b, gat_b).wait_recv()
    assemble(nblk, gat_b)
    nx[x] = nblk[...]
    send(14, nx_, x, line_x, lambda q: nblk, nx.at[x], nx)
    invert_in(hmat, SERVE_B)
    raw_b = -dot_full(nblk[...] * arow[...], hmat[...])
    ablk[...] = raw_b

    fac[...] = raw_b * arow[...]
    rows[...] = sum_rows(fac)
    scatter_out(part_c, rows)
    recv_c[me_c] = part_c[me_c]
    send(15, n_c, me_c, peer_c, lambda q: part_c.at[q], recv_c.at[me_c], recv_c)

    all_of(14, nx_, x, line_x, nx).wait_recv()
    half_n[...] = gram_of(-dot_full(nx[...].reshape(nx_ * 128, rank) * arow[...], hmat[...]))
    swap(16, half_n, other_n)
    gram = swapped(16, half_n, other_n)
    along, down = diagonals(gram)
    scale_b = jnp.sqrt(along / counts[1] + 1e-06)
    inverse_b = 1.0 / scale_b
    hmat[...] = gca[...] * ((gram * inverse_b) * (1.0 / jnp.sqrt(down / counts[1] + 1e-06)))
    ob_ref[...] = own_rows(ablk, me_b, ob_ref.shape[0]) / scale_b
    arow[...] = inverse_b
    invert_in(hmat, 0, SERVE_C)
    all_of(15, n_c, me_c, peer_c, recv_c).wait_recv()
    own_c[...] = jnp.sum(recv_c[...], axis=0)
    gat_c[ia] = own_c[...]
    send(17, ni, ia, line_i, lambda q: own_c, gat_c.at[ia], gat_c)
    invert_in(hmat, SERVE_C)

    all_of(17, ni, ia, line_i, gat_c).wait_recv()
    per = own_c.shape[0]
    assemble(fac.at[pl.ds(0, ni * per)], gat_c)
    raw_c = -dot_full(fac[0 : ni * per, :] * arow[...], hmat[...])
    squares = jnp.sum(raw_c * raw_c, axis=0, keepdims=True)
    own_n[...] = squares
    nrm[me_a] = squares
    send(18, n_a, me_a, peer_a, lambda q: own_n, nrm.at[me_a], nrm)
    mine_c = raw_c[0:per]
    for t in range(1, ni):
        mine_c = jnp.where(ia == t, raw_c[t * per : (t + 1) * per], mine_c)
    all_of(18, n_a, me_a, peer_a, nrm).wait_recv()
    squares = jnp.sum(nrm[...], axis=0)
    oc_ref[...] = mine_c / jnp.sqrt(squares / counts[2] + 1e-06)

    for phase, n, me, peer, buf in started:
        all_of(phase, n, me, peer, buf).wait_send()


def per_device(ni, nj, nk, tensor, factor_b, factor_c):
    counts = (tensor.shape[0] * ni, tensor.shape[1] * nj, tensor.shape[2] * nk)
    rank = factor_b.shape[1]
    n_a, n_b, n_c, n_x = nj * nk, ni * nk, ni * nj, nj // 2
    r_a, r_b, r_c = 128 // n_a, 128 // n_b, 128 // n_c
    v = lambda *shape: pltpu.VMEM(shape, F32)
    square = v(rank, rank)
    scratch = [
        v(16384, 128), pltpu.VMEM((16384, 256), BF16), v(16384, rank),
        v(ni, nk, r_b, rank), v(ni, nj, r_c, rank),
        v(128, rank), v(128, rank), v(128, rank), v(128, rank),
        pltpu.VMEM((256, rank), BF16), pltpu.VMEM((256, rank), BF16),
        v(128, rank), v(128, rank), v(1, rank),
        v(n_a, r_a, rank), v(n_b, r_b, rank), v(n_c, r_c, rank),
        v(n_a, r_a, rank), v(n_b, r_b, rank), v(n_c, r_c, rank),
        v(r_a, rank), v(r_b, rank), v(r_c, rank),
        v(n_a, r_a, rank), v(n_b, r_b, rank), v(ni, r_c, rank),
        v(n_x, 128, rank), v(nk, 64, rank), v(n_x, 128, rank),
        square, square, square, v(1, rank, rank), v(1, rank, rank), v(1, rank, rank),
        v(n_a, rank // n_a, rank), v(ni, rank // n_a, rank), v(rank // n_a, rank), v(n_a, rank // n_a, rank),
        square, square, square, v(n_a, 1, rank), v(1, rank),
        pltpu.SemaphoreType.DMA((19,)), pltpu.SemaphoreType.DMA((19,)), pltpu.SemaphoreType.DMA((3,)),
    ]
    vmem = pl.BlockSpec(memory_space=pltpu.VMEM)
    return pl.pallas_call(
        functools.partial(kernel, ni, nj, nk, counts),
        out_shape=(
            jax.ShapeDtypeStruct((r_a, rank), F32),
            jax.ShapeDtypeStruct((r_b, rank), F32),
            jax.ShapeDtypeStruct((r_c, rank), F32),
        ),
        in_specs=[pl.BlockSpec(memory_space=pl.ANY)] * 3,
        out_specs=(vmem, vmem, vmem),
        scratch_shapes=scratch,
        compiler_params=pltpu.CompilerParams(
            collective_id=0, has_side_effects=True, vmem_limit_bytes=52 * 1024 * 1024
        ),
    )(tensor.reshape(16384, 128), factor_b, factor_c)


def solution(mesh):
    ni, nj, nk = mesh.shape["ia"], mesh.shape["ja"], mesh.shape["ka"]
    return jax.shard_map(
        functools.partial(per_device, ni, nj, nk),
        mesh=mesh,
        in_specs=(P("ia", "ja", "ka"), P(("ja", "ia", "ka"), None), P(("ka", "ia", "ja"), None)),
        out_specs=(
            P(("ia", "ja", "ka"), None),
            P(("ja", "ia", "ka"), None),
            P(("ka", "ia", "ja"), None),
        ),
        check_vma=False,
    )
```

```python
import functools

import jax
import jax.numpy as jnp
from jax import lax
from jax.experimental import pallas as pl
from jax.experimental.pallas import tpu as pltpu
from jax.sharding import PartitionSpec as P

MESH = pl.DeviceIdType.MESH
F32 = jnp.float32
BF16 = jnp.bfloat16
HIGHEST = lax.Precision.HIGHEST
PIV = 64
BLOCK = 16
GROUP = 32
SERVE = 2
SERVE_B = 2
SERVE_C = 1
TURNS = (48, 96)


def split(v):
    hi = v.astype(BF16)
    lo = (v - hi.astype(F32)).astype(BF16)
    return hi, lo


def stack_split(v):
    hi, lo = split(v)
    return jnp.concatenate([hi, hi], axis=0), jnp.concatenate([lo, lo], axis=0)


def mxu(left, right):
    return jnp.dot(left, right, preferred_element_type=F32)


def dot_full(left, right):
    return jnp.dot(left, right, preferred_element_type=F32, precision=HIGHEST)


def gram_of(rows):
    return lax.dot_general(
        rows, rows, (((0,), (0,)), ((), ())), preferred_element_type=F32, precision=HIGHEST
    )


def diagonals(matrix):
    n = matrix.shape[0]
    row = lax.broadcasted_iota(jnp.int32, (n, n), 0)
    col = lax.broadcasted_iota(jnp.int32, (n, n), 1)
    only = jnp.where(row == col, matrix, 0.0)
    return jnp.sum(only, axis=0, keepdims=True), jnp.sum(only, axis=1, keepdims=True)


def row_of(v, r):
    return jnp.broadcast_to(v[r : r + 1, :], v.shape)


def pivot_block(groups, first):
    n = groups[0].shape[1]
    sub = lax.broadcasted_iota(jnp.int32, (8, 128), 0)
    lane = lax.broadcasted_iota(jnp.int32, (8, 128), 1)
    cols = [[jnp.broadcast_to(g[:, first + j : first + j + 1], (8, 128)) for g in groups] for j in range(BLOCK)]
    parts = [[g[:, h : h + 128] for g in groups] for h in range(0, n, 128)]
    for p in range(BLOCK):
        group, r = p // 8, p % 8
        here = sub == r
        inverse = 1.0 / row_of(cols[p][group], r)
        factor = [v * inverse for v in cols[p]]
        factor[group] = jnp.where(here, 1.0 - inverse, factor[group])
        parts[0] = [
            jnp.where(lane == first + p, jnp.where(here, 1.0, 0.0) if g == group else 0.0, v)
            for g, v in enumerate(parts[0])
        ]

        def eliminate(vs):
            row = row_of(vs[group], r)
            return [v - f * row for v, f in zip(vs, factor)]

        for j in range(p + 1, BLOCK):
            cols[j] = eliminate(cols[j])
        parts = [eliminate(vs) for vs in parts]
    return [jnp.concatenate(vs, axis=1) for vs in zip(*parts)]


def pivot_panel(front):
    n = front.shape[1]
    size = BLOCK // 8
    groups = [front[g : g + 8, :] for g in range(0, PIV, 8)]
    lane = lax.broadcasted_iota(jnp.int32, (8, n), 1)
    blocks = PIV // BLOCK
    for t in range(blocks):
        own = list(range(t * size, t * size + size))
        others = [g for g in range(len(groups)) if g not in own]
        near = others if t == blocks - 1 else [g for g in others if own[-1] < g <= own[-1] + size]
        far = [g for g in others if g not in near]
        first = t * BLOCK
        cols = {
            g: [jnp.broadcast_to(groups[g][:, first + j : first + j + 1], (8, 128)) for j in range(BLOCK)]
            for g in near
        }
        new = pivot_block([groups[g] for g in own], first)
        wide = [row_of(new[j // 8], j % 8) for j in range(BLOCK)]
        inside = (lane >= first) & (lane < first + BLOCK)
        before = list(groups)
        for g, v in zip(own, new):
            groups[g] = v
        for g in near:
            halves = []
            for h in range(0, n, 128):
                terms = [cols[g][j] * wide[j][:, h : h + 128] for j in range(BLOCK)]
                while len(terms) > 1:
                    terms = [terms[i] + terms[i + 1] for i in range(0, len(terms), 2)]
                halves.append(terms[0])
            groups[g] = jnp.where(inside, 0.0, before[g]) - jnp.concatenate(halves, axis=1)
        if far:
            left = jnp.concatenate([jnp.where(inside, before[g], 0.0)[:, 0:128] for g in far], axis=0)
            right = ([jnp.zeros((first, n), F32)] if first else []) + new + [jnp.zeros((128 - first - BLOCK, n), F32)]
            product = dot_full(left, jnp.concatenate(right, axis=0))
            for i, g in enumerate(far):
                groups[g] = jnp.where(inside, 0.0, before[g]) - product[8 * i : 8 * i + 8, :]
    return jnp.concatenate(groups, axis=0)


def sweep_step(mat):
    n = mat.shape[0]
    panel = pivot_panel(mat[0:PIV, :])
    lane = lax.broadcasted_iota(jnp.int32, (PIV, n), 1)
    rest_lane = lax.broadcasted_iota(jnp.int32, (n - PIV, n), 1)
    panel_wide = jnp.concatenate([panel, jnp.zeros((128 - PIV, n), F32)], axis=0)
    left = jnp.where(rest_lane[:, 0:128] < PIV, mat[PIV:, 0:128], 0.0)
    rest = mat[PIV:, :] - dot_full(left, panel_wide)
    tall = jnp.concatenate([panel_wide.T[PIV:, :], jnp.zeros((n - PIV, n - 128), F32)], axis=1)
    rest = jnp.where(rest_lane < PIV, tall, rest)
    top = jnp.where(lane < PIV, -panel, panel)
    return pltpu.roll(jnp.concatenate([rest, top], axis=0), n - PIV, 1)


def invert_in(ref, first=0, last=None):
    def step(_, carry):
        ref[...] = sweep_step(ref[...])
        return carry

    lax.fori_loop(first, ref.shape[0] // PIV if last is None else last, step, 0)


def unit_diagonal(matrix):
    along, down = diagonals(matrix)
    along, down = 1.0 / jnp.sqrt(along), 1.0 / jnp.sqrt(down)
    return (matrix * along) * down, along


def kernel(
    ni, nj, nk, counts,
    x_hbm, b_hbm, c_hbm, oa_ref, ob_ref, oc_ref,
    xs, xt, ys, bin_, cin, bblk, cblk, ablk, nblk, whi, wlo, rows, fac, arow, hrow,
    part_a, part_b, part_c, recv_a, recv_b, recv_c, own_a, own_b, own_c, gat_a, gat_b, gat_c,
    bx, cy, nx, half_b, half_c, half_n, other_b, other_c, other_n,
    gp_a, ex_a, sum_a, g_a, gcm, hmat, gca, nrm, own_n,
    ss, rs, xsem,
):
    rank = b_hbm.shape[1]
    nblkrows = 128
    ia, ja, ka = lax.axis_index("ia"), lax.axis_index("ja"), lax.axis_index("ka")
    n_a, n_b, n_c, nx_ = nj * nk, ni * nk, ni * nj, nj // 2
    me_a, me_b, me_c = ja * nk + ka, ia * nk + ka, ia * nj + ja
    x, core = ja // 2, lax.rem(ja, 2)

    def peer_a(q):
        return {"ia": ia, "ja": q // nk, "ka": lax.rem(q, nk)}

    def peer_b(q):
        return {"ia": q // nk, "ja": ja, "ka": lax.rem(q, nk)}

    def peer_c(q):
        return {"ia": q // nj, "ja": lax.rem(q, nj), "ka": ka}

    def line_i(q):
        return {"ia": q, "ja": ja, "ka": ka}

    def line_j(q):
        return {"ia": ia, "ja": q, "ka": ka}

    def line_k(q):
        return {"ia": ia, "ja": ja, "ka": q}

    started = []

    def line_x(q):
        return {"ia": ia, "ja": q * 2 + core, "ka": ka}

    def sibling(q):
        return {"ia": ia, "ja": x * 2 + q, "ka": ka}

    def send(phase, n, me, peer, src_of, dst, buf):
        started.append((phase, n, me, peer, buf))

        def go(p, carry):
            q = lax.rem(me + p, n)
            pltpu.make_async_remote_copy(
                src_ref=src_of(q), dst_ref=dst, send_sem=ss.at[phase], recv_sem=rs.at[phase],
                device_id=peer(q), device_id_type=MESH,
            ).start()
            return carry
        lax.fori_loop(1, n, go, 0)

    def all_of(phase, n, me, peer, buf):
        some = buf.at[pl.ds(0, n - 1)]
        return pltpu.make_async_remote_copy(
            src_ref=some, dst_ref=some, send_sem=ss.at[phase], recv_sem=rs.at[phase],
            device_id=peer(lax.rem(me + 1, n)), device_id_type=MESH,
        )

    def assemble(dst, src):
        per = src.shape[-2]
        count = dst.shape[0] // per
        outer = src.shape[0]
        for s in range(count):
            dst[s * per : (s + 1) * per, :] = src[s] if len(src.shape) == 3 else src[s % outer, s // outer]

    def scatter_out(dst, src):
        n, per = dst.shape[0], dst.shape[1]
        for s in range(n):
            dst[s] = src[s * per : (s + 1) * per, :]

    def own_rows(blk, me, per):
        if per >= 8:
            return blk[pl.ds(pl.multiple_of(me * per, 8), per), :]
        shared = 8 // per
        tile = blk[pl.ds(pl.multiple_of(me // shared * 8, 8), 8), :]
        mine = tile[0:per]
        for t in range(1, shared):
            mine = jnp.where(lax.rem(me, shared) == t, tile[t * per : (t + 1) * per], mine)
        return mine

    def solve(summed):
        return dot_full(summed * hrow[...], hmat[...]) * -hrow[...]

    xcopy = pltpu.make_async_copy(x_hbm, xs, xsem.at[0])
    xcopy.start()
    bcopy = pltpu.make_async_copy(b_hbm, bin_.at[ka, ia], xsem.at[1])
    bcopy.start()
    ccopy = pltpu.make_async_copy(c_hbm, cin.at[ja, ia], xsem.at[2])
    ccopy.start()
    barrier = pltpu.get_barrier_semaphore()

    def hello(n, me, peer):
        def go(p, carry):
            pl.semaphore_signal(barrier, inc=1, device_id=peer(lax.rem(me + p, n)), device_id_type=MESH)
            return carry
        lax.fori_loop(1, n, go, 0)

    hello(ni, ia, line_i)
    hello(nj, ja, line_j)
    hello(nk, ka, line_k)

    def turn(j, carry):
        hi, lo = split(xs[pl.ds(j, nblkrows, stride=nblkrows), :].T)
        at = pl.ds(pl.multiple_of(j * nblkrows, nblkrows), nblkrows)
        xt[at, 0:128] = hi
        xt[at, 128:256] = lo
        return carry

    def turn_some(first, last):
        lax.fori_loop(first, last, turn, 0, unroll=16)

    bcopy.wait()
    ccopy.wait()
    xcopy.wait()
    turn_some(0, TURNS[0])
    pl.semaphore_wait(barrier, ni + nj + nk - 3)

    send(0, ni, ia, line_i, lambda q: bin_.at[ka, ia], bin_.at[ka, ia], bin_.at[ka])
    send(1, ni, ia, line_i, lambda q: cin.at[ja, ia], cin.at[ja, ia], cin.at[ja])
    turn_some(TURNS[0], TURNS[1])
    all_of(0, ni, ia, line_i, bin_.at[ka]).wait_recv()
    send(2, nk, ka, line_k, lambda q: bin_.at[ka], bin_.at[ka], bin_)
    all_of(1, ni, ia, line_i, cin.at[ja]).wait_recv()
    send(3, nj, ja, line_j, lambda q: cin.at[ja], cin.at[ja], cin)
    turn_some(TURNS[1], 128)
    all_of(2, nk, ka, line_k, bin_).wait_recv()
    assemble(bblk, bin_)
    bx[x] = bblk[...]
    send(4, nx_, x, line_x, lambda q: bblk, bx.at[x], bx)
    all_of(3, nj, ja, line_j, cin).wait_recv()
    assemble(cblk, cin)
    mine = pl.ds(pl.multiple_of(core * 64, 64), 64)
    cy[ka] = cblk[mine, :]
    send(5, nk, ka, line_k, lambda q: cblk.at[mine], cy.at[ka], cy)

    def gram_slices(dst, blk):
        dst[...] = gram_of(blk[...]).reshape(dst.shape)

    whi[...], wlo[...] = stack_split(cblk[...])
    step_rows = GROUP * nblkrows

    def mode_one(g, carry):
        at = pl.ds(pl.multiple_of(g * step_rows, step_rows), step_rows)
        hi, lo = split(xs[at, :])
        both = jnp.concatenate([hi, lo], axis=1)
        y = mxu(both, whi[...]) + mxu(both, wlo[...])
        ys[at, :] = y
        terms = y.reshape(GROUP, nblkrows, rank) * bblk[...][None]
        rows[pl.ds(pl.multiple_of(g * GROUP, GROUP), GROUP), :] = jnp.sum(terms, axis=1)
        return carry

    steps = 128 // GROUP
    lax.fori_loop(0, steps, mode_one, 0)

    scatter_out(part_a, rows)
    recv_a[me_a] = part_a[me_a]
    send(6, n_a, me_a, peer_a, lambda q: part_a.at[q], recv_a.at[me_a], recv_a)

    def swap(phase, half, other):
        send(phase, 2, core, sibling, lambda q: half, other.at[0], other)

    def swapped(phase, half, other):
        all_of(phase, 2, core, sibling, other).wait_recv()
        return half[...] + other[0]

    all_of(5, nk, ka, line_k, cy).wait_recv()
    half_c[...] = gram_of(cy[...].reshape(nk * 64, rank))
    swap(7, half_c, other_c)
    all_of(4, nx_, x, line_x, bx).wait_recv()
    half_b[...] = gram_of(bx[...].reshape(nx_ * 128, rank))
    swap(8, half_b, other_b)
    gcm[...] = swapped(7, half_c, other_c)
    hmat[...], hrow[...] = unit_diagonal(swapped(8, half_b, other_b) * gcm[...])
    invert_in(hmat, 0, SERVE)
    all_of(6, n_a, me_a, peer_a, recv_a).wait_recv()
    own_a[...] = jnp.sum(recv_a[...], axis=0)
    gat_a[me_a] = own_a[...]
    send(9, n_a, me_a, peer_a, lambda q: own_a, gat_a.at[me_a], gat_a)
    invert_in(hmat, SERVE)

    all_of(9, n_a, me_a, peer_a, gat_a).wait_recv()
    assemble(ablk, gat_a)
    ablk[...] = solve(ablk[...])

    def sum_rows(factor):
        def add(s, total):
            at = pl.ds(pl.multiple_of(s * nblkrows, nblkrows), nblkrows)
            return total + ys[at, :] * factor[pl.ds(s, 1), :]
        return lax.fori_loop(0, 128, add, jnp.zeros((nblkrows, rank), F32), unroll=8)

    rows[...] = sum_rows(ablk)
    scatter_out(part_b, rows)
    recv_b[me_b] = part_b[me_b]
    send(12, n_b, me_b, peer_b, lambda q: part_b.at[q], recv_b.at[me_b], recv_b)

    gram_slices(gp_a, ablk)
    ex_a[ia] = gp_a[me_a]
    send(10, ni, ia, line_i, lambda q: gp_a.at[me_a], ex_a.at[ia], ex_a)

    whi[...], wlo[...] = stack_split(ablk[...])

    def third(g, carry):
        at = pl.ds(pl.multiple_of(g * step_rows, step_rows), step_rows)
        both = xt[at, :]
        ys[at, :] = mxu(both, whi[...]) + mxu(both, wlo[...])
        return carry
    lax.fori_loop(0, steps // 2, third, 0)
    all_of(10, ni, ia, line_i, ex_a).wait_recv()
    total_a = jnp.sum(ex_a[...], axis=0)
    sum_a[...] = total_a
    g_a[me_a] = total_a
    send(11, n_a, me_a, peer_a, lambda q: sum_a, g_a.at[me_a], g_a)

    lax.fori_loop(steps // 2, steps, third, 0)

    all_of(12, n_b, me_b, peer_b, recv_b).wait_recv()
    own_b[...] = jnp.sum(recv_b[...], axis=0)
    gat_b[me_b] = own_b[...]
    send(13, n_b, me_b, peer_b, lambda q: own_b, gat_b.at[me_b], gat_b)

    all_of(11, n_a, me_a, peer_a, g_a).wait_recv()
    gram = g_a[...].reshape(rank, rank)
    along, down = diagonals(gram)
    scale_a = jnp.sqrt(along / counts[0] + 1e-06)
    inverse_a = 1.0 / scale_a
    gca[...] = (gram * inverse_a) * (1.0 / jnp.sqrt(down / counts[0] + 1e-06))
    hmat[...], hrow[...] = unit_diagonal(gca[...] * gcm[...])
    oa_ref[...] = own_rows(ablk, me_a, oa_ref.shape[0]) / scale_a
    arow[...] = inverse_a
    invert_in(hmat, 0, SERVE_B)
    all_of(13, n_b, me_b, peer_b, gat_b).wait_recv()
    assemble(nblk, gat_b)
    nx[x] = nblk[...]
    send(14, nx_, x, line_x, lambda q: nblk, nx.at[x], nx)
    invert_in(hmat, SERVE_B)
    raw_b = solve(nblk[...] * arow[...])
    ablk[...] = raw_b

    fac[...] = raw_b * arow[...]
    rows[...] = sum_rows(fac)
    scatter_out(part_c, rows)
    recv_c[me_c] = part_c[me_c]
    send(15, n_c, me_c, peer_c, lambda q: part_c.at[q], recv_c.at[me_c], recv_c)

    all_of(14, nx_, x, line_x, nx).wait_recv()
    half_n[...] = gram_of(solve(nx[...].reshape(nx_ * 128, rank) * arow[...]))
    swap(16, half_n, other_n)
    gram = swapped(16, half_n, other_n)
    along, down = diagonals(gram)
    scale_b = jnp.sqrt(along / counts[1] + 1e-06)
    inverse_b = 1.0 / scale_b
    hmat[...], hrow[...] = unit_diagonal(gca[...] * ((gram * inverse_b) * (1.0 / jnp.sqrt(down / counts[1] + 1e-06))))
    ob_ref[...] = own_rows(ablk, me_b, ob_ref.shape[0]) / scale_b
    arow[...] = inverse_b
    invert_in(hmat, 0, SERVE_C)
    all_of(15, n_c, me_c, peer_c, recv_c).wait_recv()
    own_c[...] = jnp.sum(recv_c[...], axis=0)
    gat_c[ia] = own_c[...]
    send(17, ni, ia, line_i, lambda q: own_c, gat_c.at[ia], gat_c)
    invert_in(hmat, SERVE_C)

    all_of(17, ni, ia, line_i, gat_c).wait_recv()
    per = own_c.shape[0]
    assemble(fac.at[pl.ds(0, ni * per)], gat_c)
    raw_c = solve(fac[0 : ni * per, :] * arow[...])
    squares = jnp.sum(raw_c * raw_c, axis=0, keepdims=True)
    own_n[...] = squares
    nrm[me_a] = squares
    send(18, n_a, me_a, peer_a, lambda q: own_n, nrm.at[me_a], nrm)
    mine_c = raw_c[0:per]
    for t in range(1, ni):
        mine_c = jnp.where(ia == t, raw_c[t * per : (t + 1) * per], mine_c)
    all_of(18, n_a, me_a, peer_a, nrm).wait_recv()
    squares = jnp.sum(nrm[...], axis=0)
    oc_ref[...] = mine_c / jnp.sqrt(squares / counts[2] + 1e-06)

    for phase, n, me, peer, buf in started:
        all_of(phase, n, me, peer, buf).wait_send()


def per_device(ni, nj, nk, tensor, factor_b, factor_c):
    counts = (tensor.shape[0] * ni, tensor.shape[1] * nj, tensor.shape[2] * nk)
    rank = factor_b.shape[1]
    n_a, n_b, n_c, n_x = nj * nk, ni * nk, ni * nj, nj // 2
    r_a, r_b, r_c = 128 // n_a, 128 // n_b, 128 // n_c
    v = lambda *shape: pltpu.VMEM(shape, F32)
    square = v(rank, rank)
    scratch = [
        v(16384, 128), pltpu.VMEM((16384, 256), BF16), v(16384, rank),
        v(nk, ni, r_b, rank), v(nj, ni, r_c, rank),
        v(128, rank), v(128, rank), v(128, rank), v(128, rank),
        pltpu.VMEM((256, rank), BF16), pltpu.VMEM((256, rank), BF16),
        v(128, rank), v(128, rank), v(1, rank), v(1, rank),
        v(n_a, r_a, rank), v(n_b, r_b, rank), v(n_c, r_c, rank),
        v(n_a, r_a, rank), v(n_b, r_b, rank), v(n_c, r_c, rank),
        v(r_a, rank), v(r_b, rank), v(r_c, rank),
        v(n_a, r_a, rank), v(n_b, r_b, rank), v(ni, r_c, rank),
        v(n_x, 128, rank), v(nk, 64, rank), v(n_x, 128, rank),
        square, square, square, v(1, rank, rank), v(1, rank, rank), v(1, rank, rank),
        v(n_a, rank // n_a, rank), v(ni, rank // n_a, rank), v(rank // n_a, rank), v(n_a, rank // n_a, rank),
        square, square, square, v(n_a, 1, rank), v(1, rank),
        pltpu.SemaphoreType.DMA((19,)), pltpu.SemaphoreType.DMA((19,)), pltpu.SemaphoreType.DMA((3,)),
    ]
    vmem = pl.BlockSpec(memory_space=pltpu.VMEM)
    return pl.pallas_call(
        functools.partial(kernel, ni, nj, nk, counts),
        out_shape=(
            jax.ShapeDtypeStruct((r_a, rank), F32),
            jax.ShapeDtypeStruct((r_b, rank), F32),
            jax.ShapeDtypeStruct((r_c, rank), F32),
        ),
        in_specs=[pl.BlockSpec(memory_space=pl.ANY)] * 3,
        out_specs=(vmem, vmem, vmem),
        scratch_shapes=scratch,
        compiler_params=pltpu.CompilerParams(
            collective_id=0, has_side_effects=True, vmem_limit_bytes=52 * 1024 * 1024
        ),
    )(tensor.reshape(16384, 128), factor_b, factor_c)


def solution(mesh):
    ni, nj, nk = mesh.shape["ia"], mesh.shape["ja"], mesh.shape["ka"]
    return jax.shard_map(
        functools.partial(per_device, ni, nj, nk),
        mesh=mesh,
        in_specs=(P("ia", "ja", "ka"), P(("ja", "ia", "ka"), None), P(("ka", "ia", "ja"), None)),
        out_specs=(
            P(("ia", "ja", "ka"), None),
            P(("ja", "ia", "ka"), None),
            P(("ka", "ia", "ja"), None),
        ),
        check_vma=False,
    )
```

```python
import functools

import jax
import jax.numpy as jnp
from jax import lax
from jax.experimental import pallas as pl
from jax.experimental.pallas import tpu as pltpu
from jax.sharding import PartitionSpec as P

MESH = pl.DeviceIdType.MESH
F32 = jnp.float32
BF16 = jnp.bfloat16
HIGHEST = lax.Precision.HIGHEST
PIV = 64
BLOCK = 16
GROUP = 32
SERVE = 2
SERVE_B = 2
SERVE_C = 1
TURNS = 80


def split(v):
    hi = v.astype(BF16)
    lo = (v - hi.astype(F32)).astype(BF16)
    return hi, lo


def stack_split(v):
    hi, lo = split(v)
    return jnp.concatenate([hi, hi], axis=0), jnp.concatenate([lo, lo], axis=0)


def mxu(left, right):
    return jnp.dot(left, right, preferred_element_type=F32)


def dot_full(left, right):
    return jnp.dot(left, right, preferred_element_type=F32, precision=HIGHEST)


def gram_of(rows):
    return lax.dot_general(
        rows, rows, (((0,), (0,)), ((), ())), preferred_element_type=F32, precision=HIGHEST
    )


def diagonals(matrix):
    n = matrix.shape[0]
    row = lax.broadcasted_iota(jnp.int32, (n, n), 0)
    col = lax.broadcasted_iota(jnp.int32, (n, n), 1)
    only = jnp.where(row == col, matrix, 0.0)
    return jnp.sum(only, axis=0, keepdims=True), jnp.sum(only, axis=1, keepdims=True)


def row_of(v, r):
    return jnp.broadcast_to(v[r : r + 1, :], v.shape)


def pivot_block(groups, first):
    n = groups[0].shape[1]
    sub = lax.broadcasted_iota(jnp.int32, (8, 128), 0)
    lane = lax.broadcasted_iota(jnp.int32, (8, 128), 1)
    cols = [[jnp.broadcast_to(g[:, first + j : first + j + 1], (8, 128)) for g in groups] for j in range(BLOCK)]
    parts = [[g[:, h : h + 128] for g in groups] for h in range(0, n, 128)]
    for p in range(BLOCK):
        group, r = p // 8, p % 8
        here = sub == r
        inverse = 1.0 / row_of(cols[p][group], r)
        factor = [v * inverse for v in cols[p]]
        factor[group] = jnp.where(here, 1.0 - inverse, factor[group])
        parts[0] = [
            jnp.where(lane == first + p, jnp.where(here, 1.0, 0.0) if g == group else 0.0, v)
            for g, v in enumerate(parts[0])
        ]

        def eliminate(vs):
            row = row_of(vs[group], r)
            return [v - f * row for v, f in zip(vs, factor)]

        for j in range(p + 1, BLOCK):
            cols[j] = eliminate(cols[j])
        parts = [eliminate(vs) for vs in parts]
    return [jnp.concatenate(vs, axis=1) for vs in zip(*parts)]


def pivot_panel(front):
    n = front.shape[1]
    size = BLOCK // 8
    groups = [front[g : g + 8, :] for g in range(0, PIV, 8)]
    lane = lax.broadcasted_iota(jnp.int32, (8, n), 1)
    blocks = PIV // BLOCK
    for t in range(blocks):
        own = list(range(t * size, t * size + size))
        others = [g for g in range(len(groups)) if g not in own]
        near = others if t == blocks - 1 else [g for g in others if own[-1] < g <= own[-1] + size]
        far = [g for g in others if g not in near]
        first = t * BLOCK
        cols = {
            g: [jnp.broadcast_to(groups[g][:, first + j : first + j + 1], (8, 128)) for j in range(BLOCK)]
            for g in near
        }
        new = pivot_block([groups[g] for g in own], first)
        wide = [row_of(new[j // 8], j % 8) for j in range(BLOCK)]
        inside = (lane >= first) & (lane < first + BLOCK)
        before = list(groups)
        for g, v in zip(own, new):
            groups[g] = v
        for g in near:
            halves = []
            for h in range(0, n, 128):
                terms = [cols[g][j] * wide[j][:, h : h + 128] for j in range(BLOCK)]
                while len(terms) > 1:
                    terms = [terms[i] + terms[i + 1] for i in range(0, len(terms), 2)]
                halves.append(terms[0])
            groups[g] = jnp.where(inside, 0.0, before[g]) - jnp.concatenate(halves, axis=1)
        if far:
            left = jnp.concatenate([jnp.where(inside, before[g], 0.0)[:, 0:128] for g in far], axis=0)
            right = ([jnp.zeros((first, n), F32)] if first else []) + new + [jnp.zeros((128 - first - BLOCK, n), F32)]
            product = dot_full(left, jnp.concatenate(right, axis=0))
            for i, g in enumerate(far):
                groups[g] = jnp.where(inside, 0.0, before[g]) - product[8 * i : 8 * i + 8, :]
    return jnp.concatenate(groups, axis=0)


def sweep_step(mat):
    n = mat.shape[0]
    panel = pivot_panel(mat[0:PIV, :])
    lane = lax.broadcasted_iota(jnp.int32, (PIV, n), 1)
    rest_lane = lax.broadcasted_iota(jnp.int32, (n - PIV, n), 1)
    panel_wide = jnp.concatenate([panel, jnp.zeros((128 - PIV, n), F32)], axis=0)
    left = jnp.where(rest_lane[:, 0:128] < PIV, mat[PIV:, 0:128], 0.0)
    rest = mat[PIV:, :] - dot_full(left, panel_wide)
    tall = jnp.concatenate([panel_wide.T[PIV:, :], jnp.zeros((n - PIV, n - 128), F32)], axis=1)
    rest = jnp.where(rest_lane < PIV, tall, rest)
    top = jnp.where(lane < PIV, -panel, panel)
    return pltpu.roll(jnp.concatenate([rest, top], axis=0), n - PIV, 1)


def invert_in(ref, first=0, last=None):
    def step(_, carry):
        ref[...] = sweep_step(ref[...])
        return carry

    lax.fori_loop(first, ref.shape[0] // PIV if last is None else last, step, 0)


def unit_diagonal(matrix):
    along, down = diagonals(matrix)
    along, down = 1.0 / jnp.sqrt(along), 1.0 / jnp.sqrt(down)
    return (matrix * along) * down, along


def kernel(
    ni, nj, nk, counts,
    x_hbm, b_hbm, c_hbm, out_ref,
    xs, xt, ys, bin_, cin, bblk, cblk, ablk, nblk, whi, wlo, rows, fac, arow, hrow,
    part_a, part_b, part_c, recv_a, recv_b, recv_c, own_a, own_b, own_c, gat_a, gat_b, gat_c,
    bx, cy, nx, half_b, half_c, half_n, other_b, other_c, other_n,
    gp_a, ex_a, sum_a, g_a, gcm, hmat, gca, nrm, own_n,
    ss, rs, xsem,
):
    rank = b_hbm.shape[1]
    nblkrows = 128
    ia, ja, ka = lax.axis_index("ia"), lax.axis_index("ja"), lax.axis_index("ka")
    n_a, n_b, n_c, nx_ = nj * nk, ni * nk, ni * nj, nj // 2
    me_a, me_b, me_c = ja * nk + ka, ia * nk + ka, ia * nj + ja
    x, core = ja // 2, lax.rem(ja, 2)

    def peer_a(q):
        return {"ia": ia, "ja": q // nk, "ka": lax.rem(q, nk)}

    def peer_b(q):
        return {"ia": q // nk, "ja": ja, "ka": lax.rem(q, nk)}

    def peer_c(q):
        return {"ia": q // nj, "ja": lax.rem(q, nj), "ka": ka}

    def line_i(q):
        return {"ia": q, "ja": ja, "ka": ka}

    def line_j(q):
        return {"ia": ia, "ja": q, "ka": ka}

    def line_k(q):
        return {"ia": ia, "ja": ja, "ka": q}

    started = []

    def line_x(q):
        return {"ia": ia, "ja": q * 2 + core, "ka": ka}

    def sibling(q):
        return {"ia": ia, "ja": x * 2 + q, "ka": ka}

    def send(phase, n, me, peer, src_of, dst, buf):
        started.append((phase, n, me, peer, buf))

        def go(p, carry):
            q = lax.rem(me + p, n)
            pltpu.make_async_remote_copy(
                src_ref=src_of(q), dst_ref=dst, send_sem=ss.at[phase], recv_sem=rs.at[phase],
                device_id=peer(q), device_id_type=MESH,
            ).start()
            return carry
        lax.fori_loop(1, n, go, 0)

    def all_of(phase, n, me, peer, buf):
        some = buf.at[pl.ds(0, n - 1)]
        return pltpu.make_async_remote_copy(
            src_ref=some, dst_ref=some, send_sem=ss.at[phase], recv_sem=rs.at[phase],
            device_id=peer(lax.rem(me + 1, n)), device_id_type=MESH,
        )

    def assemble(dst, src):
        per = src.shape[-2]
        count = dst.shape[0] // per
        outer = src.shape[0]
        for s in range(count):
            dst[s * per : (s + 1) * per, :] = src[s] if len(src.shape) == 3 else src[s % outer, s // outer]

    def scatter_out(dst, src):
        n, per = dst.shape[0], dst.shape[1]
        for s in range(n):
            dst[s] = src[s * per : (s + 1) * per, :]

    def own_rows(blk, me, per):
        if per >= 8:
            return blk[pl.ds(pl.multiple_of(me * per, 8), per), :]
        shared = 8 // per
        tile = blk[pl.ds(pl.multiple_of(me // shared * 8, 8), 8), :]
        mine = tile[0:per]
        for t in range(1, shared):
            mine = jnp.where(lax.rem(me, shared) == t, tile[t * per : (t + 1) * per], mine)
        return mine

    def solve(summed):
        return dot_full(summed * hrow[...], hmat[...]) * -hrow[...]

    xcopy = pltpu.make_async_copy(x_hbm, xs, xsem.at[0])
    xcopy.start()
    bcopy = pltpu.make_async_copy(b_hbm, bin_.at[ka, ia], xsem.at[1])
    bcopy.start()
    ccopy = pltpu.make_async_copy(c_hbm, cin.at[ja, ia], xsem.at[2])
    ccopy.start()
    barrier = pltpu.get_barrier_semaphore()

    def hello(n, me, peer):
        def go(p, carry):
            pl.semaphore_signal(barrier, inc=1, device_id=peer(lax.rem(me + p, n)), device_id_type=MESH)
            return carry
        lax.fori_loop(1, n, go, 0)

    hello(ni, ia, line_i)
    hello(nj, ja, line_j)
    hello(nk, ka, line_k)

    def turn(j, carry):
        hi, lo = split(xs[pl.ds(j, nblkrows, stride=nblkrows), :].T)
        at = pl.ds(pl.multiple_of(j * nblkrows, nblkrows), nblkrows)
        xt[at, 0:128] = hi
        xt[at, 128:256] = lo
        return carry

    def turn_some(first, last):
        lax.fori_loop(first, last, turn, 0, unroll=16)

    bcopy.wait()
    ccopy.wait()
    pl.semaphore_wait(barrier, ni + nj + nk - 3)

    send(0, ni, ia, line_i, lambda q: bin_.at[ka, ia], bin_.at[ka, ia], bin_.at[ka])
    send(1, ni, ia, line_i, lambda q: cin.at[ja, ia], cin.at[ja, ia], cin.at[ja])
    xcopy.wait()
    turn_some(0, TURNS)
    all_of(0, ni, ia, line_i, bin_.at[ka]).wait_recv()
    send(2, nk, ka, line_k, lambda q: bin_.at[ka], bin_.at[ka], bin_)
    all_of(1, ni, ia, line_i, cin.at[ja]).wait_recv()
    send(3, nj, ja, line_j, lambda q: cin.at[ja], cin.at[ja], cin)
    turn_some(TURNS, 128)
    all_of(2, nk, ka, line_k, bin_).wait_recv()
    assemble(bblk, bin_)
    bx[x] = bblk[...]
    send(4, nx_, x, line_x, lambda q: bblk, bx.at[x], bx)
    all_of(3, nj, ja, line_j, cin).wait_recv()
    assemble(cblk, cin)
    mine = pl.ds(pl.multiple_of(core * 64, 64), 64)
    cy[ka] = cblk[mine, :]
    send(5, nk, ka, line_k, lambda q: cblk.at[mine], cy.at[ka], cy)

    def gram_slices(dst, blk):
        dst[...] = gram_of(blk[...]).reshape(dst.shape)

    whi[...], wlo[...] = stack_split(cblk[...])
    step_rows = GROUP * nblkrows

    def mode_one(g, carry):
        at = pl.ds(pl.multiple_of(g * step_rows, step_rows), step_rows)
        hi, lo = split(xs[at, :])
        both = jnp.concatenate([hi, lo], axis=1)
        y = mxu(both, whi[...]) + mxu(both, wlo[...])
        ys[at, :] = y
        terms = y.reshape(GROUP, nblkrows, rank) * bblk[...][None]
        rows[pl.ds(pl.multiple_of(g * GROUP, GROUP), GROUP), :] = jnp.sum(terms, axis=1)
        return carry

    steps = 128 // GROUP
    lax.fori_loop(0, steps, mode_one, 0)

    scatter_out(part_a, rows)
    recv_a[me_a] = part_a[me_a]
    send(6, n_a, me_a, peer_a, lambda q: part_a.at[q], recv_a.at[me_a], recv_a)

    def swap(phase, half, other):
        send(phase, 2, core, sibling, lambda q: half, other.at[0], other)

    def swapped(phase, half, other):
        all_of(phase, 2, core, sibling, other).wait_recv()
        return half[...] + other[0]

    all_of(5, nk, ka, line_k, cy).wait_recv()
    half_c[...] = gram_of(cy[...].reshape(nk * 64, rank))
    swap(7, half_c, other_c)
    all_of(4, nx_, x, line_x, bx).wait_recv()
    half_b[...] = gram_of(bx[...].reshape(nx_ * 128, rank))
    swap(8, half_b, other_b)
    gcm[...] = swapped(7, half_c, other_c)
    hmat[...], hrow[...] = unit_diagonal(swapped(8, half_b, other_b) * gcm[...])
    invert_in(hmat, 0, SERVE)
    all_of(6, n_a, me_a, peer_a, recv_a).wait_recv()
    own_a[...] = jnp.sum(recv_a[...], axis=0)
    gat_a[me_a] = own_a[...]
    send(9, n_a, me_a, peer_a, lambda q: own_a, gat_a.at[me_a], gat_a)
    invert_in(hmat, SERVE)

    all_of(9, n_a, me_a, peer_a, gat_a).wait_recv()
    assemble(ablk, gat_a)
    ablk[...] = solve(ablk[...])

    gram_slices(gp_a, ablk)
    ex_a[ia] = gp_a[me_a]
    send(10, ni, ia, line_i, lambda q: gp_a.at[me_a], ex_a.at[ia], ex_a)

    def sum_rows(factor):
        def add(s, total):
            at = pl.ds(pl.multiple_of(s * nblkrows, nblkrows), nblkrows)
            return total + ys[at, :] * factor[pl.ds(s, 1), :]
        return lax.fori_loop(0, 128, add, jnp.zeros((nblkrows, rank), F32), unroll=8)

    rows[...] = sum_rows(ablk)
    scatter_out(part_b, rows)
    recv_b[me_b] = part_b[me_b]
    send(12, n_b, me_b, peer_b, lambda q: part_b.at[q], recv_b.at[me_b], recv_b)

    whi[...], wlo[...] = stack_split(ablk[...])

    def third(g, carry):
        at = pl.ds(pl.multiple_of(g * step_rows, step_rows), step_rows)
        both = xt[at, :]
        ys[at, :] = mxu(both, whi[...]) + mxu(both, wlo[...])
        return carry
    lax.fori_loop(0, steps // 2, third, 0)
    all_of(10, ni, ia, line_i, ex_a).wait_recv()
    total_a = jnp.sum(ex_a[...], axis=0)
    sum_a[...] = total_a
    g_a[me_a] = total_a
    send(11, n_a, me_a, peer_a, lambda q: sum_a, g_a.at[me_a], g_a)

    lax.fori_loop(steps // 2, steps, third, 0)

    all_of(12, n_b, me_b, peer_b, recv_b).wait_recv()
    own_b[...] = jnp.sum(recv_b[...], axis=0)
    gat_b[me_b] = own_b[...]
    send(13, n_b, me_b, peer_b, lambda q: own_b, gat_b.at[me_b], gat_b)

    all_of(11, n_a, me_a, peer_a, g_a).wait_recv()
    gram = g_a[...].reshape(rank, rank)
    along, down = diagonals(gram)
    scale_a = jnp.sqrt(along / counts[0] + 1e-06)
    inverse_a = 1.0 / scale_a
    gca[...] = (gram * inverse_a) * (1.0 / jnp.sqrt(down / counts[0] + 1e-06))
    hmat[...], hrow[...] = unit_diagonal(gca[...] * gcm[...])
    r_a, r_b, r_c = own_a.shape[0], own_b.shape[0], own_c.shape[0]
    out_ref[0:r_a, :] = own_rows(ablk, me_a, r_a) / scale_a
    arow[...] = inverse_a
    invert_in(hmat, 0, SERVE_B)
    all_of(13, n_b, me_b, peer_b, gat_b).wait_recv()
    assemble(nblk, gat_b)
    nx[x] = nblk[...]
    send(14, nx_, x, line_x, lambda q: nblk, nx.at[x], nx)
    invert_in(hmat, SERVE_B)
    raw_b = solve(nblk[...] * arow[...])
    ablk[...] = raw_b

    fac[...] = raw_b * arow[...]
    rows[...] = sum_rows(fac)
    scatter_out(part_c, rows)
    recv_c[me_c] = part_c[me_c]
    send(15, n_c, me_c, peer_c, lambda q: part_c.at[q], recv_c.at[me_c], recv_c)

    all_of(14, nx_, x, line_x, nx).wait_recv()
    half_n[...] = gram_of(solve(nx[...].reshape(nx_ * 128, rank) * arow[...]))
    swap(16, half_n, other_n)
    gram = swapped(16, half_n, other_n)
    along, down = diagonals(gram)
    scale_b = jnp.sqrt(along / counts[1] + 1e-06)
    inverse_b = 1.0 / scale_b
    hmat[...], hrow[...] = unit_diagonal(gca[...] * ((gram * inverse_b) * (1.0 / jnp.sqrt(down / counts[1] + 1e-06))))
    out_ref[r_a : r_a + r_b, :] = own_rows(ablk, me_b, r_b) / scale_b
    arow[...] = inverse_b
    invert_in(hmat, 0, SERVE_C)
    all_of(15, n_c, me_c, peer_c, recv_c).wait_recv()
    own_c[...] = jnp.sum(recv_c[...], axis=0)
    gat_c[ia] = own_c[...]
    send(17, ni, ia, line_i, lambda q: own_c, gat_c.at[ia], gat_c)
    invert_in(hmat, SERVE_C)

    all_of(17, ni, ia, line_i, gat_c).wait_recv()
    per = own_c.shape[0]
    assemble(fac.at[pl.ds(0, ni * per)], gat_c)
    raw_c = solve(fac[0 : ni * per, :] * arow[...])
    squares = jnp.sum(raw_c * raw_c, axis=0, keepdims=True)
    own_n[...] = squares
    nrm[me_a] = squares
    send(18, n_a, me_a, peer_a, lambda q: own_n, nrm.at[me_a], nrm)
    mine_c = raw_c[0:per]
    for t in range(1, ni):
        mine_c = jnp.where(ia == t, raw_c[t * per : (t + 1) * per], mine_c)
    all_of(18, n_a, me_a, peer_a, nrm).wait_recv()
    squares = jnp.sum(nrm[...], axis=0)
    out_ref[r_a + r_b : r_a + r_b + r_c, :] = mine_c / jnp.sqrt(squares / counts[2] + 1e-06)

    for phase, n, me, peer, buf in started:
        all_of(phase, n, me, peer, buf).wait_send()


def part_outputs(in_ref, *out_refs):
    first = 0
    for ref in out_refs:
        ref[...] = in_ref[first : first + ref.shape[0], :]
        first += ref.shape[0]


def per_device(ni, nj, nk, tensor, factor_b, factor_c):
    counts = (tensor.shape[0] * ni, tensor.shape[1] * nj, tensor.shape[2] * nk)
    rank = factor_b.shape[1]
    n_a, n_b, n_c, n_x = nj * nk, ni * nk, ni * nj, nj // 2
    r_a, r_b, r_c = 128 // n_a, 128 // n_b, 128 // n_c
    v = lambda *shape: pltpu.VMEM(shape, F32)
    square = v(rank, rank)
    scratch = [
        v(16384, 128), pltpu.VMEM((16384, 256), BF16), v(16384, rank),
        v(nk, ni, r_b, rank), v(nj, ni, r_c, rank),
        v(128, rank), v(128, rank), v(128, rank), v(128, rank),
        pltpu.VMEM((256, rank), BF16), pltpu.VMEM((256, rank), BF16),
        v(128, rank), v(128, rank), v(1, rank), v(1, rank),
        v(n_a, r_a, rank), v(n_b, r_b, rank), v(n_c, r_c, rank),
        v(n_a, r_a, rank), v(n_b, r_b, rank), v(n_c, r_c, rank),
        v(r_a, rank), v(r_b, rank), v(r_c, rank),
        v(n_a, r_a, rank), v(n_b, r_b, rank), v(ni, r_c, rank),
        v(n_x, 128, rank), v(nk, 64, rank), v(n_x, 128, rank),
        square, square, square, v(1, rank, rank), v(1, rank, rank), v(1, rank, rank),
        v(n_a, rank // n_a, rank), v(ni, rank // n_a, rank), v(rank // n_a, rank), v(n_a, rank // n_a, rank),
        square, square, square, v(n_a, 1, rank), v(1, rank),
        pltpu.SemaphoreType.DMA((19,)), pltpu.SemaphoreType.DMA((19,)), pltpu.SemaphoreType.DMA((3,)),
    ]
    vmem = pl.BlockSpec(memory_space=pltpu.VMEM)
    stacked = pl.pallas_call(
        functools.partial(kernel, ni, nj, nk, counts),
        out_shape=jax.ShapeDtypeStruct((r_a + r_b + r_c, rank), F32),
        in_specs=[pl.BlockSpec(memory_space=pl.ANY)] * 3,
        out_specs=vmem,
        scratch_shapes=scratch,
        compiler_params=pltpu.CompilerParams(
            collective_id=0, has_side_effects=True, vmem_limit_bytes=60 * 1024 * 1024
        ),
    )(tensor.reshape(16384, 128), factor_b, factor_c)
    return pl.pallas_call(
        part_outputs,
        out_shape=tuple(jax.ShapeDtypeStruct((r, rank), F32) for r in (r_a, r_b, r_c)),
        in_specs=[vmem],
        out_specs=(vmem, vmem, vmem),
    )(stacked)


def solution(mesh):
    ni, nj, nk = mesh.shape["ia"], mesh.shape["ja"], mesh.shape["ka"]
    return jax.shard_map(
        functools.partial(per_device, ni, nj, nk),
        mesh=mesh,
        in_specs=(P("ia", "ja", "ka"), P(("ja", "ia", "ka"), None), P(("ka", "ia", "ja"), None)),
        out_specs=(
            P(("ia", "ja", "ka"), None),
            P(("ja", "ia", "ka"), None),
            P(("ka", "ia", "ja"), None),
        ),
        check_vma=False,
    )
```

```python
import functools

import jax
import jax.numpy as jnp
from jax import lax
from jax.experimental import pallas as pl
from jax.experimental.pallas import tpu as pltpu
from jax.sharding import PartitionSpec as P

MESH = pl.DeviceIdType.MESH
F32 = jnp.float32
BF16 = jnp.bfloat16
HIGHEST = lax.Precision.HIGHEST
PIV = 64
BLOCK = 16
GROUP = 32
SERVE = 1
SERVE_B = 2
SERVE_C = 1
TURNS = 80


def split(v):
    hi = v.astype(BF16)
    lo = (v - hi.astype(F32)).astype(BF16)
    return hi, lo


def stack_split(v):
    hi, lo = split(v)
    return jnp.concatenate([hi, hi], axis=0), jnp.concatenate([lo, lo], axis=0)


def mxu(left, right):
    return jnp.dot(left, right, preferred_element_type=F32)


def dot_full(left, right):
    return jnp.dot(left, right, preferred_element_type=F32, precision=HIGHEST)


def gram_of(rows):
    return lax.dot_general(
        rows, rows, (((0,), (0,)), ((), ())), preferred_element_type=F32, precision=HIGHEST
    )


def diagonals(matrix):
    n = matrix.shape[0]
    row = lax.broadcasted_iota(jnp.int32, (n, n), 0)
    col = lax.broadcasted_iota(jnp.int32, (n, n), 1)
    only = jnp.where(row == col, matrix, 0.0)
    return jnp.sum(only, axis=0, keepdims=True), jnp.sum(only, axis=1, keepdims=True)


def row_of(v, r):
    return jnp.broadcast_to(v[r : r + 1, :], v.shape)


def pivot_block(groups, first):
    n = groups[0].shape[1]
    sub = lax.broadcasted_iota(jnp.int32, (8, 128), 0)
    lane = lax.broadcasted_iota(jnp.int32, (8, 128), 1)
    cols = [[jnp.broadcast_to(g[:, first + j : first + j + 1], (8, 128)) for g in groups] for j in range(BLOCK)]
    parts = [[g[:, h : h + 128] for g in groups] for h in range(0, n, 128)]
    for p in range(BLOCK):
        group, r = p // 8, p % 8
        here = sub == r
        inverse = 1.0 / row_of(cols[p][group], r)
        factor = [v * inverse for v in cols[p]]
        factor[group] = jnp.where(here, 1.0 - inverse, factor[group])
        parts[0] = [
            jnp.where(lane == first + p, jnp.where(here, 1.0, 0.0) if g == group else 0.0, v)
            for g, v in enumerate(parts[0])
        ]

        def eliminate(vs):
            row = row_of(vs[group], r)
            return [v - f * row for v, f in zip(vs, factor)]

        for j in range(p + 1, BLOCK):
            cols[j] = eliminate(cols[j])
        parts = [eliminate(vs) for vs in parts]
    return [jnp.concatenate(vs, axis=1) for vs in zip(*parts)]


def pivot_panel(front):
    n = front.shape[1]
    size = BLOCK // 8
    groups = [front[g : g + 8, :] for g in range(0, PIV, 8)]
    lane = lax.broadcasted_iota(jnp.int32, (8, n), 1)
    blocks = PIV // BLOCK
    for t in range(blocks):
        own = list(range(t * size, t * size + size))
        others = [g for g in range(len(groups)) if g not in own]
        near = others if t == blocks - 1 else [g for g in others if own[-1] < g <= own[-1] + size]
        far = [g for g in others if g not in near]
        first = t * BLOCK
        cols = {
            g: [jnp.broadcast_to(groups[g][:, first + j : first + j + 1], (8, 128)) for j in range(BLOCK)]
            for g in near
        }
        new = pivot_block([groups[g] for g in own], first)
        wide = [row_of(new[j // 8], j % 8) for j in range(BLOCK)]
        inside = (lane >= first) & (lane < first + BLOCK)
        before = list(groups)
        for g, v in zip(own, new):
            groups[g] = v
        for g in near:
            halves = []
            for h in range(0, n, 128):
                terms = [cols[g][j] * wide[j][:, h : h + 128] for j in range(BLOCK)]
                while len(terms) > 1:
                    terms = [terms[i] + terms[i + 1] for i in range(0, len(terms), 2)]
                halves.append(terms[0])
            groups[g] = jnp.where(inside, 0.0, before[g]) - jnp.concatenate(halves, axis=1)
        if far:
            left = jnp.concatenate([jnp.where(inside, before[g], 0.0)[:, 0:128] for g in far], axis=0)
            right = ([jnp.zeros((first, n), F32)] if first else []) + new + [jnp.zeros((128 - first - BLOCK, n), F32)]
            product = dot_full(left, jnp.concatenate(right, axis=0))
            for i, g in enumerate(far):
                groups[g] = jnp.where(inside, 0.0, before[g]) - product[8 * i : 8 * i + 8, :]
    return jnp.concatenate(groups, axis=0)


def sweep_step(mat):
    n = mat.shape[0]
    panel = pivot_panel(mat[0:PIV, :])
    lane = lax.broadcasted_iota(jnp.int32, (PIV, n), 1)
    rest_lane = lax.broadcasted_iota(jnp.int32, (n - PIV, n), 1)
    panel_wide = jnp.concatenate([panel, jnp.zeros((128 - PIV, n), F32)], axis=0)
    left = jnp.where(rest_lane[:, 0:128] < PIV, mat[PIV:, 0:128], 0.0)
    rest = mat[PIV:, :] - dot_full(left, panel_wide)
    tall = jnp.concatenate([panel_wide.T[PIV:, :], jnp.zeros((n - PIV, n - 128), F32)], axis=1)
    rest = jnp.where(rest_lane < PIV, tall, rest)
    top = jnp.where(lane < PIV, -panel, panel)
    return pltpu.roll(jnp.concatenate([rest, top], axis=0), n - PIV, 1)


def invert_in(ref, first=0, last=None):
    def step(_, carry):
        ref[...] = sweep_step(ref[...])
        return carry

    lax.fori_loop(first, ref.shape[0] // PIV if last is None else last, step, 0)


def unit_diagonal(matrix):
    along, down = diagonals(matrix)
    return (matrix * (1.0 / jnp.sqrt(along))) * (1.0 / jnp.sqrt(down)), along


def kernel(
    ni, nj, nk, counts,
    x_hbm, b_hbm, c_hbm, out_ref,
    xs, xt, ys, bin_, cin, bblk, cblk, ablk, nblk, whi, wlo, rows, fac, sol_b, arow, hrow, crow, scales,
    part_a, part_b, part_c, recv_a, recv_b, recv_c, own_a, own_b, own_c, gat_a, gat_b, gat_c,
    bx, cy, nx, half_b, half_c, half_n, other_b, other_c, other_n,
    gp_a, ex_a, sum_a, g_a, gcm, hmat, gca, nrm, own_n,
    ss, rs, xsem,
):
    rank = b_hbm.shape[1]
    nblkrows = 128
    ia, ja, ka = lax.axis_index("ia"), lax.axis_index("ja"), lax.axis_index("ka")
    n_a, n_b, n_c, nx_ = nj * nk, ni * nk, ni * nj, nj // 2
    me_a, me_b, me_c = ja * nk + ka, ia * nk + ka, ia * nj + ja
    x, core = ja // 2, lax.rem(ja, 2)

    def peer_a(q):
        return {"ia": ia, "ja": q // nk, "ka": lax.rem(q, nk)}

    def peer_b(q):
        return {"ia": q // nk, "ja": ja, "ka": lax.rem(q, nk)}

    def peer_c(q):
        return {"ia": q // nj, "ja": lax.rem(q, nj), "ka": ka}

    def line_i(q):
        return {"ia": q, "ja": ja, "ka": ka}

    def line_j(q):
        return {"ia": ia, "ja": q, "ka": ka}

    def line_k(q):
        return {"ia": ia, "ja": ja, "ka": q}

    started = []

    def line_x(q):
        return {"ia": ia, "ja": q * 2 + core, "ka": ka}

    def sibling(q):
        return {"ia": ia, "ja": x * 2 + q, "ka": ka}

    def send(phase, n, me, peer, src_of, dst, buf):
        started.append((phase, n, me, peer, buf))

        def copy_to(p):
            q = lax.rem(me + p, n)
            pltpu.make_async_remote_copy(
                src_ref=src_of(q), dst_ref=dst, send_sem=ss.at[phase], recv_sem=rs.at[phase],
                device_id=peer(q), device_id_type=MESH,
            ).start()

        def both_ways(t, carry):
            copy_to(n // 2 - t)
            copy_to(n // 2 + t)
            return carry

        copy_to(n // 2)
        if n > 2:
            lax.fori_loop(1, n // 2, both_ways, 0)

    def all_of(phase, n, me, peer, buf):
        some = buf.at[pl.ds(0, n - 1)]
        return pltpu.make_async_remote_copy(
            src_ref=some, dst_ref=some, send_sem=ss.at[phase], recv_sem=rs.at[phase],
            device_id=peer(lax.rem(me + 1, n)), device_id_type=MESH,
        )

    def assemble(dst, src):
        per = src.shape[-2]
        count = dst.shape[0] // per
        outer = src.shape[0]
        for s in range(count):
            dst[s * per : (s + 1) * per, :] = src[s] if len(src.shape) == 3 else src[s % outer, s // outer]

    def scatter_out(dst, src):
        n, per = dst.shape[0], dst.shape[1]
        for s in range(n):
            dst[s] = src[s * per : (s + 1) * per, :]

    def own_rows(blk, me, per):
        if per >= 8:
            return blk[pl.ds(pl.multiple_of(me * per, 8), per), :]
        shared = 8 // per
        tile = blk[pl.ds(pl.multiple_of(me // shared * 8, 8), 8), :]
        mine = tile[0:per]
        for t in range(1, shared):
            mine = jnp.where(lax.rem(me, shared) == t, tile[t * per : (t + 1) * per], mine)
        return mine

    def solve(summed):
        return dot_full(summed * hrow[...], hmat[...]) * -hrow[...]

    xcopy = pltpu.make_async_copy(x_hbm, xs, xsem.at[0])
    xcopy.start()
    bcopy = pltpu.make_async_copy(b_hbm, bin_.at[ka, ia], xsem.at[1])
    bcopy.start()
    ccopy = pltpu.make_async_copy(c_hbm, cin.at[ja, ia], xsem.at[2])
    ccopy.start()
    barrier = pltpu.get_barrier_semaphore()

    def hello(n, me, peer):
        def go(p, carry):
            pl.semaphore_signal(barrier, inc=1, device_id=peer(lax.rem(me + p, n)), device_id_type=MESH)
            return carry
        lax.fori_loop(1, n, go, 0)

    hello(ni, ia, line_i)
    hello(nj, ja, line_j)
    hello(nk, ka, line_k)

    def turn(j, carry):
        hi, lo = split(xs[pl.ds(j, nblkrows, stride=nblkrows), :].T)
        at = pl.ds(pl.multiple_of(j * nblkrows, nblkrows), nblkrows)
        xt[at, 0:128] = hi
        xt[at, 128:256] = lo
        return carry

    def turn_some(first, last):
        lax.fori_loop(first, last, turn, 0, unroll=16)

    bcopy.wait()
    ccopy.wait()
    pl.semaphore_wait(barrier, ni + nj + nk - 3)

    send(0, ni, ia, line_i, lambda q: bin_.at[ka, ia], bin_.at[ka, ia], bin_.at[ka])
    send(1, ni, ia, line_i, lambda q: cin.at[ja, ia], cin.at[ja, ia], cin.at[ja])
    xcopy.wait()
    turn_some(0, TURNS)
    all_of(0, ni, ia, line_i, bin_.at[ka]).wait_recv()
    send(2, nk, ka, line_k, lambda q: bin_.at[ka], bin_.at[ka], bin_)
    all_of(1, ni, ia, line_i, cin.at[ja]).wait_recv()
    send(3, nj, ja, line_j, lambda q: cin.at[ja], cin.at[ja], cin)
    turn_some(TURNS, 128)
    all_of(2, nk, ka, line_k, bin_).wait_recv()
    assemble(bblk, bin_)
    bx[x] = bblk[...]
    send(4, nx_, x, line_x, lambda q: bblk, bx.at[x], bx)
    all_of(3, nj, ja, line_j, cin).wait_recv()
    assemble(cblk, cin)
    mine = pl.ds(pl.multiple_of(core * 64, 64), 64)
    cy[ka] = cblk[mine, :]
    send(5, nk, ka, line_k, lambda q: cblk.at[mine], cy.at[ka], cy)

    def gram_slices(dst, blk):
        dst[...] = gram_of(blk[...]).reshape(dst.shape)

    whi[...], wlo[...] = stack_split(cblk[...])
    step_rows = GROUP * nblkrows

    def mode_one(g, carry):
        at = pl.ds(pl.multiple_of(g * step_rows, step_rows), step_rows)
        hi, lo = split(xs[at, :])
        both = jnp.concatenate([hi, lo], axis=1)
        y = mxu(both, whi[...]) + mxu(both, wlo[...])
        ys[at, :] = y
        terms = y.reshape(GROUP, nblkrows, rank) * bblk[...][None]
        rows[pl.ds(pl.multiple_of(g * GROUP, GROUP), GROUP), :] = jnp.sum(terms, axis=1)
        return carry

    steps = 128 // GROUP
    lax.fori_loop(0, steps, mode_one, 0)

    scatter_out(part_a, rows)
    recv_a[me_a] = part_a[me_a]
    send(6, n_a, me_a, peer_a, lambda q: part_a.at[q], recv_a.at[me_a], recv_a)

    def swap(phase, half, other):
        send(phase, 2, core, sibling, lambda q: half, other.at[0], other)

    def swapped(phase, half, other):
        all_of(phase, 2, core, sibling, other).wait_recv()
        return half[...] + other[0]

    all_of(5, nk, ka, line_k, cy).wait_recv()
    half_c[...] = gram_of(cy[...].reshape(nk * 64, rank))
    swap(7, half_c, other_c)
    all_of(4, nx_, x, line_x, bx).wait_recv()
    half_b[...] = gram_of(bx[...].reshape(nx_ * 128, rank))
    swap(8, half_b, other_b)
    unit_c, diag_c = unit_diagonal(swapped(7, half_c, other_c))
    gcm[...] = unit_c
    crow[...] = 1.0 / jnp.sqrt(diag_c)
    unit_b, diag_b = unit_diagonal(swapped(8, half_b, other_b))
    hmat[...] = unit_b * gcm[...]
    hrow[...] = (1.0 / jnp.sqrt(diag_b)) * crow[...]
    invert_in(hmat, 0, SERVE)
    all_of(6, n_a, me_a, peer_a, recv_a).wait_recv()
    own_a[...] = jnp.sum(recv_a[...], axis=0)
    gat_a[me_a] = own_a[...]
    send(9, n_a, me_a, peer_a, lambda q: own_a, gat_a.at[me_a], gat_a)
    invert_in(hmat, SERVE)

    all_of(9, n_a, me_a, peer_a, gat_a).wait_recv()
    assemble(ablk, gat_a)
    ablk[...] = solve(ablk[...])

    gram_slices(gp_a, ablk)
    ex_a[ia] = gp_a[me_a]
    send(10, ni, ia, line_i, lambda q: gp_a.at[me_a], ex_a.at[ia], ex_a)

    def sum_rows(factor):
        def add(s, total):
            at = pl.ds(pl.multiple_of(s * nblkrows, nblkrows), nblkrows)
            return total + ys[at, :] * factor[pl.ds(s, 1), :]
        return lax.fori_loop(0, 128, add, jnp.zeros((nblkrows, rank), F32), unroll=8)

    rows[...] = sum_rows(ablk)
    scatter_out(part_b, rows)
    recv_b[me_b] = part_b[me_b]
    send(12, n_b, me_b, peer_b, lambda q: part_b.at[q], recv_b.at[me_b], recv_b)

    whi[...], wlo[...] = stack_split(ablk[...])

    def third(g, carry):
        at = pl.ds(pl.multiple_of(g * step_rows, step_rows), step_rows)
        both = xt[at, :]
        ys[at, :] = mxu(both, whi[...]) + mxu(both, wlo[...])
        return carry
    lax.fori_loop(0, steps // 2, third, 0)
    all_of(10, ni, ia, line_i, ex_a).wait_recv()
    total_a = jnp.sum(ex_a[...], axis=0)
    sum_a[...] = total_a
    g_a[me_a] = total_a
    send(11, n_a, me_a, peer_a, lambda q: sum_a, g_a.at[me_a], g_a)

    lax.fori_loop(steps // 2, steps, third, 0)

    all_of(12, n_b, me_b, peer_b, recv_b).wait_recv()
    own_b[...] = jnp.sum(recv_b[...], axis=0)
    gat_b[me_b] = own_b[...]
    send(13, n_b, me_b, peer_b, lambda q: own_b, gat_b.at[me_b], gat_b)

    all_of(11, n_a, me_a, peer_a, g_a).wait_recv()
    gram = g_a[...].reshape(rank, rank)
    unit_a, diag_a = unit_diagonal(gram)
    gca[...] = unit_a
    hmat[...] = unit_a * gcm[...]
    scale_a = jnp.sqrt(diag_a / counts[0] + 1e-06)
    ratio_a = scale_a / jnp.sqrt(diag_a)
    hrow[...] = ratio_a * crow[...]
    crow[...] = ratio_a
    arow[...] = 1.0 / scale_a
    scales[0:1, :] = scale_a
    invert_in(hmat, 0, SERVE_B)
    all_of(13, n_b, me_b, peer_b, gat_b).wait_recv()
    assemble(nblk, gat_b)
    nx[x] = nblk[...]
    send(14, nx_, x, line_x, lambda q: nblk, nx.at[x], nx)
    invert_in(hmat, SERVE_B)
    raw_b = solve(nblk[...] * arow[...])
    sol_b[...] = raw_b

    fac[...] = raw_b * arow[...]
    rows[...] = sum_rows(fac)
    scatter_out(part_c, rows)
    recv_c[me_c] = part_c[me_c]
    send(15, n_c, me_c, peer_c, lambda q: part_c.at[q], recv_c.at[me_c], recv_c)

    all_of(14, nx_, x, line_x, nx).wait_recv()
    half_n[...] = gram_of(solve(nx[...].reshape(nx_ * 128, rank) * arow[...]))
    swap(16, half_n, other_n)
    gram = swapped(16, half_n, other_n)
    unit_n, diag_n = unit_diagonal(gram)
    hmat[...] = gca[...] * unit_n
    scale_b = jnp.sqrt(diag_n / counts[1] + 1e-06)
    hrow[...] = crow[...] * (scale_b / jnp.sqrt(diag_n))
    arow[...] = 1.0 / scale_b
    scales[1:2, :] = scale_b
    invert_in(hmat, 0, SERVE_C)
    all_of(15, n_c, me_c, peer_c, recv_c).wait_recv()
    own_c[...] = jnp.sum(recv_c[...], axis=0)
    gat_c[ia] = own_c[...]
    send(17, ni, ia, line_i, lambda q: own_c, gat_c.at[ia], gat_c)
    invert_in(hmat, SERVE_C)

    all_of(17, ni, ia, line_i, gat_c).wait_recv()
    per = own_c.shape[0]
    assemble(fac.at[pl.ds(0, ni * per)], gat_c)
    raw_c = solve(fac[0 : ni * per, :] * arow[...])
    squares = jnp.sum(raw_c * raw_c, axis=0, keepdims=True)
    own_n[...] = squares
    nrm[me_a] = squares
    send(18, n_a, me_a, peer_a, lambda q: own_n, nrm.at[me_a], nrm)
    r_a, r_b, r_c = own_a.shape[0], own_b.shape[0], own_c.shape[0]
    out_ref[0:r_a, :] = own_rows(ablk, me_a, r_a) / scales[0:1, :]
    out_ref[r_a : r_a + r_b, :] = own_rows(sol_b, me_b, r_b) / scales[1:2, :]
    mine_c = raw_c[0:per]
    for t in range(1, ni):
        mine_c = jnp.where(ia == t, raw_c[t * per : (t + 1) * per], mine_c)
    all_of(18, n_a, me_a, peer_a, nrm).wait_recv()
    squares = jnp.sum(nrm[...], axis=0)
    out_ref[r_a + r_b : r_a + r_b + r_c, :] = mine_c / jnp.sqrt(squares / counts[2] + 1e-06)

    for phase, n, me, peer, buf in started:
        all_of(phase, n, me, peer, buf).wait_send()


def part_outputs(in_ref, *out_refs):
    first = 0
    for ref in out_refs:
        ref[...] = in_ref[first : first + ref.shape[0], :]
        first += ref.shape[0]


def per_device(ni, nj, nk, tensor, factor_b, factor_c):
    counts = (tensor.shape[0] * ni, tensor.shape[1] * nj, tensor.shape[2] * nk)
    rank = factor_b.shape[1]
    n_a, n_b, n_c, n_x = nj * nk, ni * nk, ni * nj, nj // 2
    r_a, r_b, r_c = 128 // n_a, 128 // n_b, 128 // n_c
    v = lambda *shape: pltpu.VMEM(shape, F32)
    square = v(rank, rank)
    scratch = [
        v(16384, 128), pltpu.VMEM((16384, 256), BF16), v(16384, rank),
        v(nk, ni, r_b, rank), v(nj, ni, r_c, rank),
        v(128, rank), v(128, rank), v(128, rank), v(128, rank),
        pltpu.VMEM((256, rank), BF16), pltpu.VMEM((256, rank), BF16),
        v(128, rank), v(128, rank), v(128, rank), v(1, rank), v(1, rank), v(1, rank), v(8, rank),
        v(n_a, r_a, rank), v(n_b, r_b, rank), v(n_c, r_c, rank),
        v(n_a, r_a, rank), v(n_b, r_b, rank), v(n_c, r_c, rank),
        v(r_a, rank), v(r_b, rank), v(r_c, rank),
        v(n_a, r_a, rank), v(n_b, r_b, rank), v(ni, r_c, rank),
        v(n_x, 128, rank), v(nk, 64, rank), v(n_x, 128, rank),
        square, square, square, v(1, rank, rank), v(1, rank, rank), v(1, rank, rank),
        v(n_a, rank // n_a, rank), v(ni, rank // n_a, rank), v(rank // n_a, rank), v(n_a, rank // n_a, rank),
        square, square, square, v(n_a, 1, rank), v(1, rank),
        pltpu.SemaphoreType.DMA((19,)), pltpu.SemaphoreType.DMA((19,)), pltpu.SemaphoreType.DMA((3,)),
    ]
    vmem = pl.BlockSpec(memory_space=pltpu.VMEM)
    stacked = pl.pallas_call(
        functools.partial(kernel, ni, nj, nk, counts),
        out_shape=jax.ShapeDtypeStruct((r_a + r_b + r_c, rank), F32),
        in_specs=[pl.BlockSpec(memory_space=pl.ANY)] * 3,
        out_specs=vmem,
        scratch_shapes=scratch,
        compiler_params=pltpu.CompilerParams(
            collective_id=0, has_side_effects=True, vmem_limit_bytes=60 * 1024 * 1024
        ),
    )(tensor.reshape(16384, 128), factor_b, factor_c)
    return pl.pallas_call(
        part_outputs,
        out_shape=tuple(jax.ShapeDtypeStruct((r, rank), F32) for r in (r_a, r_b, r_c)),
        in_specs=[vmem],
        out_specs=(vmem, vmem, vmem),
    )(stacked)


def solution(mesh):
    ni, nj, nk = mesh.shape["ia"], mesh.shape["ja"], mesh.shape["ka"]
    return jax.shard_map(
        functools.partial(per_device, ni, nj, nk),
        mesh=mesh,
        in_specs=(P("ia", "ja", "ka"), P(("ja", "ia", "ka"), None), P(("ka", "ia", "ja"), None)),
        out_specs=(
            P(("ia", "ja", "ka"), None),
            P(("ja", "ia", "ka"), None),
            P(("ka", "ia", "ja"), None),
        ),
        check_vma=False,
    )
```

```python
import functools

import jax
import jax.numpy as jnp
from jax import lax
from jax.experimental import pallas as pl
from jax.experimental.pallas import tpu as pltpu
from jax.sharding import PartitionSpec as P

MESH = pl.DeviceIdType.MESH
F32 = jnp.float32
BF16 = jnp.bfloat16
HIGHEST = lax.Precision.HIGHEST
PIV = 64
BLOCK = 16
GROUP = 32
SERVE = 1
SERVE_B = 2
SERVE_C = 1
TURNS = 80


def split(v):
    hi = v.astype(BF16)
    lo = (v - hi.astype(F32)).astype(BF16)
    return hi, lo


def stack_split(v):
    hi, lo = split(v)
    return jnp.concatenate([hi, hi], axis=0), jnp.concatenate([lo, lo], axis=0)


def mxu(left, right):
    return jnp.dot(left, right, preferred_element_type=F32)


def dot_full(left, right):
    return jnp.dot(left, right, preferred_element_type=F32, precision=HIGHEST)


def gram_of(rows):
    return lax.dot_general(
        rows, rows, (((0,), (0,)), ((), ())), preferred_element_type=F32, precision=HIGHEST
    )


def diagonals(matrix):
    n = matrix.shape[0]
    row = lax.broadcasted_iota(jnp.int32, (n, n), 0)
    col = lax.broadcasted_iota(jnp.int32, (n, n), 1)
    only = jnp.where(row == col, matrix, 0.0)
    return jnp.sum(only, axis=0, keepdims=True), jnp.sum(only, axis=1, keepdims=True)


def row_of(v, r):
    return jnp.broadcast_to(v[r : r + 1, :], v.shape)


def pivot_block(groups, first):
    n = groups[0].shape[1]
    sub = lax.broadcasted_iota(jnp.int32, (8, 128), 0)
    lane = lax.broadcasted_iota(jnp.int32, (8, 128), 1)
    cols = [[jnp.broadcast_to(g[:, first + j : first + j + 1], (8, 128)) for g in groups] for j in range(BLOCK)]
    parts = [[g[:, h : h + 128] for g in groups] for h in range(0, n, 128)]
    for p in range(BLOCK):
        group, r = p // 8, p % 8
        here = sub == r
        inverse = 1.0 / row_of(cols[p][group], r)
        factor = [v * inverse for v in cols[p]]
        factor[group] = jnp.where(here, 1.0 - inverse, factor[group])
        parts[0] = [
            jnp.where(lane == first + p, jnp.where(here, 1.0, 0.0) if g == group else 0.0, v)
            for g, v in enumerate(parts[0])
        ]

        def eliminate(vs):
            row = row_of(vs[group], r)
            return [v - f * row for v, f in zip(vs, factor)]

        for j in range(p + 1, BLOCK):
            cols[j] = eliminate(cols[j])
        parts = [eliminate(vs) for vs in parts]
    return [jnp.concatenate(vs, axis=1) for vs in zip(*parts)]


def pivot_panel(front):
    n = front.shape[1]
    size = BLOCK // 8
    groups = [front[g : g + 8, :] for g in range(0, PIV, 8)]
    lane = lax.broadcasted_iota(jnp.int32, (8, n), 1)
    blocks = PIV // BLOCK
    for t in range(blocks):
        own = list(range(t * size, t * size + size))
        others = [g for g in range(len(groups)) if g not in own]
        near = others if t == blocks - 1 else [g for g in others if own[-1] < g <= own[-1] + size]
        far = [g for g in others if g not in near]
        first = t * BLOCK
        cols = {
            g: [jnp.broadcast_to(groups[g][:, first + j : first + j + 1], (8, 128)) for j in range(BLOCK)]
            for g in near
        }
        new = pivot_block([groups[g] for g in own], first)
        wide = [row_of(new[j // 8], j % 8) for j in range(BLOCK)]
        inside = (lane >= first) & (lane < first + BLOCK)
        before = list(groups)
        for g, v in zip(own, new):
            groups[g] = v
        for g in near:
            halves = []
            for h in range(0, n, 128):
                terms = [cols[g][j] * wide[j][:, h : h + 128] for j in range(BLOCK)]
                while len(terms) > 1:
                    terms = [terms[i] + terms[i + 1] for i in range(0, len(terms), 2)]
                halves.append(terms[0])
            groups[g] = jnp.where(inside, 0.0, before[g]) - jnp.concatenate(halves, axis=1)
        if far:
            left = jnp.concatenate([jnp.where(inside, before[g], 0.0)[:, 0:128] for g in far], axis=0)
            right = ([jnp.zeros((first, n), F32)] if first else []) + new + [jnp.zeros((128 - first - BLOCK, n), F32)]
            product = dot_full(left, jnp.concatenate(right, axis=0))
            for i, g in enumerate(far):
                groups[g] = jnp.where(inside, 0.0, before[g]) - product[8 * i : 8 * i + 8, :]
    return jnp.concatenate(groups, axis=0)


def sweep_step(mat):
    n = mat.shape[0]
    panel = pivot_panel(mat[0:PIV, :])
    lane = lax.broadcasted_iota(jnp.int32, (PIV, n), 1)
    rest_lane = lax.broadcasted_iota(jnp.int32, (n - PIV, n), 1)
    panel_wide = jnp.concatenate([panel, jnp.zeros((128 - PIV, n), F32)], axis=0)
    left = jnp.where(rest_lane[:, 0:128] < PIV, mat[PIV:, 0:128], 0.0)
    rest = mat[PIV:, :] - dot_full(left, panel_wide)
    tall = jnp.concatenate([panel_wide.T[PIV:, :], jnp.zeros((n - PIV, n - 128), F32)], axis=1)
    rest = jnp.where(rest_lane < PIV, tall, rest)
    top = jnp.where(lane < PIV, -panel, panel)
    return pltpu.roll(jnp.concatenate([rest, top], axis=0), n - PIV, 1)


def invert_in(ref, first=0, last=None):
    def step(_, carry):
        ref[...] = sweep_step(ref[...])
        return carry

    lax.fori_loop(first, ref.shape[0] // PIV if last is None else last, step, 0)


def unit_diagonal(matrix):
    along, down = diagonals(matrix)
    return (matrix * (1.0 / jnp.sqrt(along))) * (1.0 / jnp.sqrt(down)), along


def kernel(
    ni, nj, nk, counts,
    x_hbm, b_hbm, c_hbm, out_ref,
    xs, xt, ys, bin_, cin, bblk, cblk, ablk, nblk, whi, wlo, rows, fac, sol_b, arow, hrow, crow, scales,
    part_a, part_b, part_c, recv_a, recv_b, recv_c, own_a, own_b, own_c, gat_a, gat_b, gat_c,
    bx, cy, nx, half_b, half_c, half_n, other_b, other_c, other_n,
    gp_a, ex_a, sum_a, g_a, gcm, hmat, gca, nrm, own_n,
    ss, rs, xsem,
):
    rank = b_hbm.shape[1]
    nblkrows = 128
    ia, ja, ka = lax.axis_index("ia"), lax.axis_index("ja"), lax.axis_index("ka")
    n_a, n_b, n_c, nx_ = nj * nk, ni * nk, ni * nj, nj // 2
    me_a, me_b, me_c = ja * nk + ka, ia * nk + ka, ia * nj + ja
    x, core = ja // 2, lax.rem(ja, 2)

    def peer_a(q):
        return {"ia": ia, "ja": q // nk, "ka": lax.rem(q, nk)}

    def peer_b(q):
        return {"ia": q // nk, "ja": ja, "ka": lax.rem(q, nk)}

    def peer_c(q):
        return {"ia": q // nj, "ja": lax.rem(q, nj), "ka": ka}

    def line_i(q):
        return {"ia": q, "ja": ja, "ka": ka}

    def line_j(q):
        return {"ia": ia, "ja": q, "ka": ka}

    def line_k(q):
        return {"ia": ia, "ja": ja, "ka": q}

    started = []

    def line_x(q):
        return {"ia": ia, "ja": q * 2 + core, "ka": ka}

    def sibling(q):
        return {"ia": ia, "ja": x * 2 + q, "ka": ka}

    def send(phase, n, me, peer, src_of, dst, buf):
        started.append((phase, n, me, peer, buf))

        def copy_to(p):
            q = lax.rem(me + p, n)
            pltpu.make_async_remote_copy(
                src_ref=src_of(q), dst_ref=dst, send_sem=ss.at[phase], recv_sem=rs.at[phase],
                device_id=peer(q), device_id_type=MESH,
            ).start()

        def both_ways(t, carry):
            copy_to(n // 2 - t)
            copy_to(n // 2 + t)
            return carry

        copy_to(n // 2)
        if n > 2:
            lax.fori_loop(1, n // 2, both_ways, 0, unroll=True)

    def all_of(phase, n, me, peer, buf):
        some = buf.at[pl.ds(0, n - 1)]
        return pltpu.make_async_remote_copy(
            src_ref=some, dst_ref=some, send_sem=ss.at[phase], recv_sem=rs.at[phase],
            device_id=peer(lax.rem(me + 1, n)), device_id_type=MESH,
        )

    def assemble(dst, src):
        per = src.shape[-2]
        count = dst.shape[0] // per
        outer = src.shape[0]
        for s in range(count):
            dst[s * per : (s + 1) * per, :] = src[s] if len(src.shape) == 3 else src[s % outer, s // outer]

    def scatter_out(dst, src):
        n, per = dst.shape[0], dst.shape[1]
        for s in range(n):
            dst[s] = src[s * per : (s + 1) * per, :]

    def own_rows(blk, me, per):
        if per >= 8:
            return blk[pl.ds(pl.multiple_of(me * per, 8), per), :]
        shared = 8 // per
        tile = blk[pl.ds(pl.multiple_of(me // shared * 8, 8), 8), :]
        mine = tile[0:per]
        for t in range(1, shared):
            mine = jnp.where(lax.rem(me, shared) == t, tile[t * per : (t + 1) * per], mine)
        return mine

    def solve(summed):
        return dot_full(summed * hrow[...], hmat[...]) * -hrow[...]

    xcopy = pltpu.make_async_copy(x_hbm, xs, xsem.at[0])
    xcopy.start()
    bcopy = pltpu.make_async_copy(b_hbm, bin_.at[ka, ia], xsem.at[1])
    bcopy.start()
    ccopy = pltpu.make_async_copy(c_hbm, cin.at[ja, ia], xsem.at[2])
    ccopy.start()
    barrier = pltpu.get_barrier_semaphore()

    def hello(n, me, peer):
        def signal_to(p):
            pl.semaphore_signal(barrier, inc=1, device_id=peer(lax.rem(me + p, n)), device_id_type=MESH)

        signal_to(n // 2)
        for t in range(1, n // 2):
            signal_to(n // 2 - t)
            signal_to(n // 2 + t)

    hello(ni, ia, line_i)
    hello(nj, ja, line_j)
    hello(nk, ka, line_k)

    def turn(j, carry):
        hi, lo = split(xs[pl.ds(j, nblkrows, stride=nblkrows), :].T)
        at = pl.ds(pl.multiple_of(j * nblkrows, nblkrows), nblkrows)
        xt[at, 0:128] = hi
        xt[at, 128:256] = lo
        return carry

    def turn_some(first, last):
        lax.fori_loop(first, last, turn, 0, unroll=16)

    bcopy.wait()
    ccopy.wait()
    pl.semaphore_wait(barrier, ni + nj + nk - 3)

    send(0, ni, ia, line_i, lambda q: bin_.at[ka, ia], bin_.at[ka, ia], bin_.at[ka])
    send(1, ni, ia, line_i, lambda q: cin.at[ja, ia], cin.at[ja, ia], cin.at[ja])
    xcopy.wait()
    turn_some(0, TURNS)
    all_of(0, ni, ia, line_i, bin_.at[ka]).wait_recv()
    send(2, nk, ka, line_k, lambda q: bin_.at[ka], bin_.at[ka], bin_)
    all_of(1, ni, ia, line_i, cin.at[ja]).wait_recv()
    send(3, nj, ja, line_j, lambda q: cin.at[ja], cin.at[ja], cin)
    turn_some(TURNS, 128)
    all_of(2, nk, ka, line_k, bin_).wait_recv()
    assemble(bblk, bin_)
    bx[x] = bblk[...]
    send(4, nx_, x, line_x, lambda q: bblk, bx.at[x], bx)
    all_of(3, nj, ja, line_j, cin).wait_recv()
    assemble(cblk, cin)
    mine = pl.ds(pl.multiple_of(core * 64, 64), 64)
    cy[ka] = cblk[mine, :]
    send(5, nk, ka, line_k, lambda q: cblk.at[mine], cy.at[ka], cy)

    def gram_slices(dst, blk):
        dst[...] = gram_of(blk[...]).reshape(dst.shape)

    whi[...], wlo[...] = stack_split(cblk[...])
    step_rows = GROUP * nblkrows

    def mode_one(g, carry):
        at = pl.ds(pl.multiple_of(g * step_rows, step_rows), step_rows)
        hi, lo = split(xs[at, :])
        both = jnp.concatenate([hi, lo], axis=1)
        y = mxu(both, whi[...]) + mxu(both, wlo[...])
        ys[at, :] = y
        terms = y.reshape(GROUP, nblkrows, rank) * bblk[...][None]
        rows[pl.ds(pl.multiple_of(g * GROUP, GROUP), GROUP), :] = jnp.sum(terms, axis=1)
        return carry

    steps = 128 // GROUP
    lax.fori_loop(0, steps, mode_one, 0)

    scatter_out(part_a, rows)
    recv_a[me_a] = part_a[me_a]
    send(6, n_a, me_a, peer_a, lambda q: part_a.at[q], recv_a.at[me_a], recv_a)

    def swap(phase, half, other):
        send(phase, 2, core, sibling, lambda q: half, other.at[0], other)

    def swapped(phase, half, other):
        all_of(phase, 2, core, sibling, other).wait_recv()
        return half[...] + other[0]

    all_of(5, nk, ka, line_k, cy).wait_recv()
    half_c[...] = gram_of(cy[...].reshape(nk * 64, rank))
    swap(7, half_c, other_c)
    all_of(4, nx_, x, line_x, bx).wait_recv()
    half_b[...] = gram_of(bx[...].reshape(nx_ * 128, rank))
    swap(8, half_b, other_b)
    unit_c, diag_c = unit_diagonal(swapped(7, half_c, other_c))
    gcm[...] = unit_c
    crow[...] = 1.0 / jnp.sqrt(diag_c)
    unit_b, diag_b = unit_diagonal(swapped(8, half_b, other_b))
    hmat[...] = unit_b * gcm[...]
    hrow[...] = (1.0 / jnp.sqrt(diag_b)) * crow[...]
    invert_in(hmat, 0, SERVE)
    all_of(6, n_a, me_a, peer_a, recv_a).wait_recv()
    own_a[...] = jnp.sum(recv_a[...], axis=0)
    gat_a[me_a] = own_a[...]
    send(9, n_a, me_a, peer_a, lambda q: own_a, gat_a.at[me_a], gat_a)
    invert_in(hmat, SERVE)

    all_of(9, n_a, me_a, peer_a, gat_a).wait_recv()
    assemble(ablk, gat_a)
    ablk[...] = solve(ablk[...])

    gram_slices(gp_a, ablk)
    ex_a[ia] = gp_a[me_a]
    send(10, ni, ia, line_i, lambda q: gp_a.at[me_a], ex_a.at[ia], ex_a)

    def sum_rows(factor):
        def add(s, total):
            at = pl.ds(pl.multiple_of(s * nblkrows, nblkrows), nblkrows)
            return total + ys[at, :] * factor[pl.ds(s, 1), :]
        return lax.fori_loop(0, 128, add, jnp.zeros((nblkrows, rank), F32), unroll=8)

    rows[...] = sum_rows(ablk)
    scatter_out(part_b, rows)
    recv_b[me_b] = part_b[me_b]
    send(12, n_b, me_b, peer_b, lambda q: part_b.at[q], recv_b.at[me_b], recv_b)

    whi[...], wlo[...] = stack_split(ablk[...])

    def third(g, carry):
        at = pl.ds(pl.multiple_of(g * step_rows, step_rows), step_rows)
        both = xt[at, :]
        ys[at, :] = mxu(both, whi[...]) + mxu(both, wlo[...])
        return carry
    lax.fori_loop(0, steps // 2, third, 0)
    all_of(10, ni, ia, line_i, ex_a).wait_recv()
    total_a = jnp.sum(ex_a[...], axis=0)
    sum_a[...] = total_a
    g_a[me_a] = total_a
    send(11, n_a, me_a, peer_a, lambda q: sum_a, g_a.at[me_a], g_a)

    lax.fori_loop(steps // 2, steps, third, 0)

    all_of(12, n_b, me_b, peer_b, recv_b).wait_recv()
    own_b[...] = jnp.sum(recv_b[...], axis=0)
    gat_b[me_b] = own_b[...]
    send(13, n_b, me_b, peer_b, lambda q: own_b, gat_b.at[me_b], gat_b)

    all_of(11, n_a, me_a, peer_a, g_a).wait_recv()
    gram = g_a[...].reshape(rank, rank)
    unit_a, diag_a = unit_diagonal(gram)
    gca[...] = unit_a
    hmat[...] = unit_a * gcm[...]
    scale_a = jnp.sqrt(diag_a / counts[0] + 1e-06)
    ratio_a = scale_a / jnp.sqrt(diag_a)
    hrow[...] = ratio_a * crow[...]
    crow[...] = ratio_a
    arow[...] = 1.0 / scale_a
    scales[0:1, :] = scale_a
    invert_in(hmat, 0, SERVE_B)
    all_of(13, n_b, me_b, peer_b, gat_b).wait_recv()
    assemble(nblk, gat_b)
    nx[x] = nblk[...]
    send(14, nx_, x, line_x, lambda q: nblk, nx.at[x], nx)
    invert_in(hmat, SERVE_B)
    raw_b = solve(nblk[...] * arow[...])
    sol_b[...] = raw_b

    fac[...] = raw_b * arow[...]
    rows[...] = sum_rows(fac)
    scatter_out(part_c, rows)
    recv_c[me_c] = part_c[me_c]
    send(15, n_c, me_c, peer_c, lambda q: part_c.at[q], recv_c.at[me_c], recv_c)

    all_of(14, nx_, x, line_x, nx).wait_recv()
    half_n[...] = gram_of(solve(nx[...].reshape(nx_ * 128, rank) * arow[...]))
    swap(16, half_n, other_n)
    gram = swapped(16, half_n, other_n)
    unit_n, diag_n = unit_diagonal(gram)
    hmat[...] = gca[...] * unit_n
    scale_b = jnp.sqrt(diag_n / counts[1] + 1e-06)
    hrow[...] = crow[...] * (scale_b / jnp.sqrt(diag_n))
    arow[...] = 1.0 / scale_b
    scales[1:2, :] = scale_b
    invert_in(hmat, 0, SERVE_C)
    all_of(15, n_c, me_c, peer_c, recv_c).wait_recv()
    own_c[...] = jnp.sum(recv_c[...], axis=0)
    gat_c[ia] = own_c[...]
    send(17, ni, ia, line_i, lambda q: own_c, gat_c.at[ia], gat_c)
    invert_in(hmat, SERVE_C)

    all_of(17, ni, ia, line_i, gat_c).wait_recv()
    per = own_c.shape[0]
    assemble(fac.at[pl.ds(0, ni * per)], gat_c)
    raw_c = solve(fac[0 : ni * per, :] * arow[...])
    squares = jnp.sum(raw_c * raw_c, axis=0, keepdims=True)
    own_n[...] = squares
    nrm[me_a] = squares
    send(18, n_a, me_a, peer_a, lambda q: own_n, nrm.at[me_a], nrm)
    r_a, r_b, r_c = own_a.shape[0], own_b.shape[0], own_c.shape[0]
    out_ref[0:r_a, :] = own_rows(ablk, me_a, r_a) / scales[0:1, :]
    out_ref[r_a : r_a + r_b, :] = own_rows(sol_b, me_b, r_b) / scales[1:2, :]
    mine_c = raw_c[0:per]
    for t in range(1, ni):
        mine_c = jnp.where(ia == t, raw_c[t * per : (t + 1) * per], mine_c)
    all_of(18, n_a, me_a, peer_a, nrm).wait_recv()
    squares = jnp.sum(nrm[...], axis=0)
    out_ref[r_a + r_b : r_a + r_b + r_c, :] = mine_c / jnp.sqrt(squares / counts[2] + 1e-06)

    for phase, n, me, peer, buf in started:
        all_of(phase, n, me, peer, buf).wait_send()


def part_outputs(in_ref, *out_refs):
    first = 0
    for ref in out_refs:
        ref[...] = in_ref[first : first + ref.shape[0], :]
        first += ref.shape[0]


def per_device(ni, nj, nk, tensor, factor_b, factor_c):
    counts = (tensor.shape[0] * ni, tensor.shape[1] * nj, tensor.shape[2] * nk)
    rank = factor_b.shape[1]
    n_a, n_b, n_c, n_x = nj * nk, ni * nk, ni * nj, nj // 2
    r_a, r_b, r_c = 128 // n_a, 128 // n_b, 128 // n_c
    v = lambda *shape: pltpu.VMEM(shape, F32)
    square = v(rank, rank)
    scratch = [
        v(16384, 128), pltpu.VMEM((16384, 256), BF16), v(16384, rank),
        v(nk, ni, r_b, rank), v(nj, ni, r_c, rank),
        v(128, rank), v(128, rank), v(128, rank), v(128, rank),
        pltpu.VMEM((256, rank), BF16), pltpu.VMEM((256, rank), BF16),
        v(128, rank), v(128, rank), v(128, rank), v(1, rank), v(1, rank), v(1, rank), v(8, rank),
        v(n_a, r_a, rank), v(n_b, r_b, rank), v(n_c, r_c, rank),
        v(n_a, r_a, rank), v(n_b, r_b, rank), v(n_c, r_c, rank),
        v(r_a, rank), v(r_b, rank), v(r_c, rank),
        v(n_a, r_a, rank), v(n_b, r_b, rank), v(ni, r_c, rank),
        v(n_x, 128, rank), v(nk, 64, rank), v(n_x, 128, rank),
        square, square, square, v(1, rank, rank), v(1, rank, rank), v(1, rank, rank),
        v(n_a, rank // n_a, rank), v(ni, rank // n_a, rank), v(rank // n_a, rank), v(n_a, rank // n_a, rank),
        square, square, square, v(n_a, 1, rank), v(1, rank),
        pltpu.SemaphoreType.DMA((19,)), pltpu.SemaphoreType.DMA((19,)), pltpu.SemaphoreType.DMA((3,)),
    ]
    vmem = pl.BlockSpec(memory_space=pltpu.VMEM)
    stacked = pl.pallas_call(
        functools.partial(kernel, ni, nj, nk, counts),
        out_shape=jax.ShapeDtypeStruct((r_a + r_b + r_c, rank), F32),
        in_specs=[pl.BlockSpec(memory_space=pl.ANY)] * 3,
        out_specs=vmem,
        scratch_shapes=scratch,
        compiler_params=pltpu.CompilerParams(
            collective_id=0, has_side_effects=True, vmem_limit_bytes=60 * 1024 * 1024
        ),
    )(tensor.reshape(16384, 128), factor_b, factor_c)
    return pl.pallas_call(
        part_outputs,
        out_shape=tuple(jax.ShapeDtypeStruct((r, rank), F32) for r in (r_a, r_b, r_c)),
        in_specs=[vmem],
        out_specs=(vmem, vmem, vmem),
    )(stacked)


def solution(mesh):
    ni, nj, nk = mesh.shape["ia"], mesh.shape["ja"], mesh.shape["ka"]
    return jax.shard_map(
        functools.partial(per_device, ni, nj, nk),
        mesh=mesh,
        in_specs=(P("ia", "ja", "ka"), P(("ja", "ia", "ka"), None), P(("ka", "ia", "ja"), None)),
        out_specs=(
            P(("ia", "ja", "ka"), None),
            P(("ja", "ia", "ka"), None),
            P(("ka", "ia", "ja"), None),
        ),
        check_vma=False,
    )
```
